128 devices in a mesh: row: 16 (over x, z), col: 8 (over y, core).
Axes of the slice: x: 4, y: 4, z: 4, core: 2. Of those that a mesh axis runs over, the one named last changes fastest.
Arguments:
- tokens: bfloat16 [16384, 8192], P('row', 'col'), may hold values from -6 to 6
- weights: bfloat16 [4, 112, 128, 256], P(None, 'col', 'row'), may hold values from -0.25 to 0.25
- block_rows: int32 [4, 112], P(None, 'col'), may hold values from 0 to 63, as said below
- grad_hidden: bfloat16 [16384, 14336], P('row', 'col'), may hold values from -6 to 6
Outputs:
- hidden: bfloat16 [16384, 14336], P(('row', 'col'))
- grad_tokens: bfloat16 [16384, 8192], P(('row', 'col'))
- grad_weights: bfloat16 [4, 112, 128, 256], P(None, 'col', 'row')
The draws below stay inside these ranges and needn't reach their ends.
Inputs may be any that keep to these rules, and one draw needn't show every extreme that they name: `block_rows`: block row indices; an index may appear more than once in a block column, and then both blocks add.
All inputs are finite; a program needn't handle non-finite values.
Results may differ from the reference program's by a relative error of at most 0.018.
Values may be sent and summed in bfloat16 or wider, within the bound.
A program may use at most 192 MiB of HBM per device.

```python
from functools import partial
import jax
import jax.numpy as jnp
from jax import lax

D = 8192
FF = 14336
BLOCK = 128
K_NZ = 4
TOK_DEV = 1024
TOKENS = 16384
N_COL = 8


def draw_block_rows(key, part):
    key = jax.random.fold_in(key, 11)
    nblocks = D // BLOCK
    ncols = FF // BLOCK
    first_key, second_key, third_key = jax.random.split(key, 3)
    order = jax.random.permutation(first_key, nblocks).astype(jnp.int32)
    octets = max(nblocks // 8, 1)
    octet_order = jax.random.permutation(third_key, octets).astype(jnp.int32)
    columns = jnp.arange(ncols, dtype=jnp.int32)
    pair_index = columns // 2 % octets
    base = (8 * octet_order[pair_index] + 7 * (columns % 2)) % nblocks
    levels = min(K_NZ, max(nblocks - 1, 1).bit_length() + 1)
    picked = []
    for level in range(levels):
        stride = 0 if level == 0 else 2 ** (level - 1)
        partner = jnp.bitwise_xor(base, stride) % nblocks
        picked.append(order[partner])
    extra = jax.random.randint(second_key, (K_NZ - levels, ncols), 0, nblocks).astype(jnp.int32)
    return jnp.concatenate([jnp.stack(picked, axis=0), extra], axis=0).astype(jnp.int32)


def steps_of(key, shape, cuts, least, high):
    loudness, own = 1.0, jax.random.fold_in(key, 6)
    for axis_at, parts in cuts:
        heights = jnp.exp(jax.random.uniform(jax.random.fold_in(own, axis_at), (parts,), jnp.float32, least / len(cuts), high / len(cuts)))
        loudness = loudness * jnp.repeat(heights, shape[axis_at] // parts).reshape([-1 if axis == axis_at else 1 for axis in range(len(shape))])
    return loudness


def scatter_about(rng, extent, width, reach, pieces=(), held_as=jnp.bfloat16):
    level = steps_of(rng, extent, pieces, -0.22, 0.18) if pieces else 1.0
    result = jax.random.normal(rng, extent, jnp.float32) * width * level
    return jnp.minimum(jnp.maximum(result, -reach), reach).astype(held_as)


def setup_inputs(seed: int = 0) -> dict:
    streams_of = jax.random.split(jax.random.key(seed), 5)
    tokens = scatter_about(streams_of[0], (TOKENS, D), 1.0, 6.0, ((0, 16), (1, 8)))
    weights = scatter_about(streams_of[1], (K_NZ, FF // BLOCK, BLOCK, 2 * BLOCK), (K_NZ * BLOCK) ** -0.5, 0.25, ((1, 8), (2, 16)))
    block_rows = draw_block_rows(jax.random.fold_in(streams_of[4], 71), 0)
    grad_hidden = scatter_about(streams_of[3], (TOKENS, FF), 1.0, 6.0, ((0, 16), (1, 8)))
    return {"tokens": tokens, "weights": weights, "block_rows": block_rows, "grad_hidden": grad_hidden}


def block_step(wide, block_rows, carry, inputs):
    tok_blk, grad_blk = inputs
    rows = tok_blk.shape[0]
    nblocks = D // BLOCK
    ncols = FF // BLOCK
    per_group = ncols // N_COL
    blocked = tok_blk.reshape(rows, nblocks, BLOCK)
    picked = blocked[:, block_rows, :].astype(jnp.float32)
    joined = jnp.einsum('tkjc,kjcf->tjf', picked, wide)
    gate = joined[:, :, :BLOCK]
    upper = joined[:, :, BLOCK:]
    hidden = (jax.nn.silu(gate) * upper).astype(jnp.bfloat16).reshape(rows, FF)
    grad = grad_blk.astype(jnp.float32).reshape(rows, ncols, BLOCK)
    sig = jax.nn.sigmoid(gate)
    grad_gate = (grad * upper * sig * (1.0 + gate * (1.0 - sig))).astype(jnp.bfloat16)
    grad_up = (grad * gate * sig).astype(jnp.bfloat16)
    grad_joined = jnp.concatenate([grad_gate, grad_up], axis=2).astype(jnp.float32)
    spread = jnp.einsum('tjf,kjcf->tkjc', grad_joined, wide)
    spread_groups = spread.reshape(rows, K_NZ, N_COL, per_group, BLOCK)
    rows_groups = block_rows.reshape(K_NZ, N_COL, per_group)
    total = jnp.zeros((nblocks, rows, BLOCK), jnp.float32)
    for group in range(N_COL):
        flat = jnp.transpose(spread_groups[:, :, group], (1, 2, 0, 3)).reshape(K_NZ * per_group, rows, BLOCK)
        summed = jax.ops.segment_sum(flat, rows_groups[:, group].reshape(-1), num_segments=nblocks)
        summed = lax.optimization_barrier(summed.astype(jnp.bfloat16))
        total = total + summed.astype(jnp.float32)
    grad_tok = jnp.transpose(total, (1, 0, 2)).reshape(rows, D).astype(jnp.bfloat16)
    partial_w = jnp.einsum('tkjc,tjf->kjcf', picked, grad_joined).astype(jnp.bfloat16)
    partial_w = lax.optimization_barrier(partial_w)
    carry = carry + partial_w.astype(jnp.float32)
    return carry, (hidden, grad_tok)


def reference(tokens, weights, block_rows, grad_hidden):
    wide = weights.astype(jnp.float32)
    nblk = TOKENS // TOK_DEV
    tok3 = tokens.reshape(nblk, TOK_DEV, D)
    grad3 = grad_hidden.reshape(nblk, TOK_DEV, FF)
    start = jnp.zeros((K_NZ, FF // BLOCK, BLOCK, 2 * BLOCK), jnp.float32)
    total, (hidden, grad_tok) = lax.scan(partial(block_step, wide, block_rows), start, (tok3, grad3))
    return hidden.reshape(TOKENS, FF), grad_tok.reshape(TOKENS, D), total.astype(jnp.bfloat16)
```

```python
import jax
import jax.numpy as jnp
from jax import lax
from jax.experimental import pallas as pl
from jax.experimental.pallas import tpu as pltpu
from jax.sharding import PartitionSpec as P

MESH = pl.DeviceIdType.MESH
BF, F32 = jnp.bfloat16, jnp.float32
ANY = pl.BlockSpec(memory_space=pl.ANY)
VMEM = pl.BlockSpec(memory_space=pltpu.VMEM)


def place():
    row, col = lax.axis_index("row"), lax.axis_index("col")
    return row // 4, row % 4, col // 2, col % 2


def at(x, z, y, core):
    return (x * 4 + z, y * 2 + core)


def greet(peers):
    barrier = pltpu.get_barrier_semaphore()
    for peer in peers:
        pl.semaphore_signal(barrier, inc=1, device_id=peer, device_id_type=MESH)
    pl.semaphore_wait(barrier, len(peers))


class Wires:
    def __init__(self, send, recv):
        self.send, self.recv, self.made = send, recv, 0

    def copy(self, src, dst, peer):
        i = self.made
        self.made += 1
        c = pltpu.make_async_remote_copy(
            src_ref=src,
            dst_ref=dst,
            send_sem=self.send.at[i],
            recv_sem=self.recv.at[i],
            device_id=peer,
            device_id_type=MESH,
        )
        c.start()
        return c


def gather_kernel(tok_ref, wv_ref, gh_ref, br_ref, tok, wide, ghb, brb, wp, slab, send, recv, local):
    x, z, y, core = place()
    col = y * 2 + core
    e, zh = z % 2, z // 2
    yp, ym, y2 = (y + 1) % 4, (y + 3) % 4, (y + 2) % 4
    zp, zm, z2 = (z + 1) % 4, (z + 3) % 4, (z + 2) % 4
    xp, xm, x2 = (x + 1) % 4, (x + 3) % 4, (x + 2) % 4
    sib = at(x, z, y, 1 - core)
    cols = [(col + d) % 8 for d in range(1, 8)]
    col_peers = [at(x, z, c // 2, c % 2) for c in cols]
    x_peers = [at(v, z, y, core) for v in (xp, xm, x2)]
    z_peers = [at(x, v, y, core) for v in (zp, zm, z2)]
    y_peers = [at(x, z, v, core) for v in (yp, ym, y2)]
    greet(col_peers + x_peers + z_peers)
    wires = Wires(send, recv)
    go = wires.copy
    pending = []

    def lcopy(src, dst, i):
        c = pltpu.make_async_copy(src, dst, local.at[i])
        c.start()
        return c

    pair = go(wv_ref.at[1 - e], wp, at(x, z + 1 - 2 * e, y, core))
    own_tok = [
        lcopy(tok_ref.at[:, pl.ds(m * 128, 128)], tok.at[y, core, m // 4, m % 4], m) for m in range(8)
    ]
    own_gh = lcopy(gh_ref.at[pl.ds(pl.multiple_of(col * 128, 128), 128)], ghb.at[col], 8)
    own_br = lcopy(br_ref, brb.at[col], 9)
    pending += [go(br_ref, brb.at[col], p) for p in col_peers]
    pair.wait_recv()
    mine, other = wv_ref[e].astype(F32), wp[...].astype(F32)
    low = jnp.where(e == 0, mine, other)
    high = jnp.where(e == 0, other, mine)
    gate = jnp.concatenate([low[:, :8], high[:, :8]], axis=1).astype(BF)
    upper = jnp.concatenate([low[:, 8:], high[:, 8:]], axis=1).astype(BF)
    slab[:, :, :, :128] = gate.reshape(2, 14, 16, 128)
    slab[:, :, :, 128:] = upper.reshape(2, 14, 16, 128)
    own_w = lcopy(slab, wide.at[y, core, e, :, :, x, zh], 10)
    ystage = [go(slab, wide.at[y, core, e, :, :, x, zh], p) for p in y_peers]
    for c in own_tok:
        c.wait()
    up, down = at(x, z, yp, core), at(x, z, ym, core)

    def tsend(yy, h, peer):
        part = tok.at[yy, core, h]
        return go(part, part, peer)

    ta_up, tb_dn = tsend(y, 0, up), tsend(y, 1, down)
    sib_copies = [tsend(y, 0, sib), tsend(y, 1, sib)]
    own_w.wait()
    for c in ystage:
        c.wait_recv()
    pending += [pair] + ystage
    first = []
    for p in x_peers:
        part = wide.at[:, core, e, 0, :, x, zh]
        first.append(go(part, part, p))
    for p in z_peers:
        part = wide.at[:, core, e, 1, :, x, zh]
        first.append(go(part, part, p))
    ta_up.wait_send()
    tb_dn.wait_send()
    tb_up, ta_dn = tsend(y, 1, up), tsend(y, 0, down)
    for c in first:
        c.wait_recv()

    def w0(zz, h):
        return wide.at[pl.ds(2 * h, 2), core, zz % 2, 0, :, :, zz // 2]

    def w1(xx, h):
        return wide.at[pl.ds(2 * h, 2), core, :, 1, :, xx]

    zup, zdn = at(x, zp, y, core), at(x, zm, y, core)
    xup, xdn = at(xp, z, y, core), at(xm, z, y, core)

    def wsend(part, peer):
        return go(part, part, peer)

    a0u, b0d = wsend(w0(z, 0), zup), wsend(w0(z, 1), zdn)
    a1u, b1d = wsend(w1(x, 0), xup), wsend(w1(x, 1), xdn)
    sib_copies += [wsend(w0(z, 0), sib), wsend(w0(z, 1), sib), wsend(w1(x, 0), sib), wsend(w1(x, 1), sib)]
    ta_up.wait_recv()
    ta_fwd = tsend(ym, 0, up)
    tb_dn.wait_recv()
    tb_fwd = tsend(yp, 1, down)
    sib_copies += [tsend(ym, 0, sib), tsend(yp, 1, sib)]
    a0u.wait_send()
    b0d.wait_send()
    b0u, a0d = wsend(w0(z, 1), zup), wsend(w0(z, 0), zdn)
    a1u.wait_send()
    b1d.wait_send()
    b1u, a1d = wsend(w1(x, 1), xup), wsend(w1(x, 0), xdn)
    ghs = [
        go(gh_ref.at[pl.ds(pl.multiple_of(c * 128, 128), 128)], ghb.at[col], p)
        for c, p in zip(cols, col_peers)
    ]
    a0u.wait_recv()
    a0f = wsend(w0(zm, 0), zup)
    b0d.wait_recv()
    b0f = wsend(w0(zp, 1), zdn)
    a1u.wait_recv()
    a1f = wsend(w1(xm, 0), xup)
    b1d.wait_recv()
    b1f = wsend(w1(xp, 1), xdn)
    sib_copies += [
        wsend(w0(zm, 0), sib),
        wsend(w0(zp, 1), sib),
        wsend(w1(xm, 0), sib),
        wsend(w1(xp, 1), sib),
    ]
    tb_up.wait_recv()
    ta_dn.wait_recv()
    sib_copies += [tsend(ym, 1, sib), tsend(yp, 0, sib)]
    b0u.wait_recv()
    a0d.wait_recv()
    b1u.wait_recv()
    a1d.wait_recv()
    sib_copies += [
        wsend(w0(zm, 1), sib),
        wsend(w0(zp, 0), sib),
        wsend(w1(xm, 1), sib),
        wsend(w1(xp, 0), sib),
    ]
    ta_fwd.wait_recv()
    tb_fwd.wait_recv()
    sib_copies += [tsend(y2, 0, sib), tsend(y2, 1, sib)]
    a0f.wait_recv()
    b0f.wait_recv()
    a1f.wait_recv()
    b1f.wait_recv()
    sib_copies += [
        wsend(w0(z2, 0), sib),
        wsend(w0(z2, 1), sib),
        wsend(w1(x2, 0), sib),
        wsend(w1(x2, 1), sib),
    ]
    own_gh.wait()
    own_br.wait()
    for c in sib_copies + ghs + pending[:7]:
        c.wait_recv()
    rest = [tb_up, ta_dn, ta_fwd, tb_fwd, b0u, a0d, b1u, a1d, a0f, b0f, a1f, b1f]
    for c in sib_copies + ghs + pending + first + rest:
        c.wait_send()


def gather_all(tokens, wv, grad_hidden, br):
    return pl.pallas_call(
        gather_kernel,
        out_shape=(
            jax.ShapeDtypeStruct((4, 2, 2, 4, 1024, 128), BF),
            jax.ShapeDtypeStruct((4, 2, 2, 2, 14, 4, 2, 16, 256), BF),
            jax.ShapeDtypeStruct((8, 128, 1792), BF),
            jax.ShapeDtypeStruct((8, 8, 128), jnp.int32),
        ),
        in_specs=[ANY, VMEM, ANY, ANY],
        out_specs=(ANY, ANY, ANY, ANY),
        scratch_shapes=[
            pltpu.VMEM((28, 16, 128), BF),
            pltpu.VMEM((2, 14, 16, 256), BF),
            pltpu.SemaphoreType.DMA((66,)),
            pltpu.SemaphoreType.DMA((66,)),
            pltpu.SemaphoreType.DMA((11,)),
        ],
        compiler_params=pltpu.CompilerParams(
            collective_id=1, has_side_effects=True, vmem_limit_bytes=16 << 20
        ),
        name="gather",
    )(tokens, wv, grad_hidden, br)


def views(weights, block_rows):
    wv = weights.reshape(4, 14, 8, 2, 128).transpose(0, 1, 3, 2, 4).reshape(2, 28, 16, 128)
    br = jnp.pad(block_rows, ((0, 4), (0, 114)))
    return wv, br


def swish_parts(joined, grad):
    gate, upper = joined[:, :128], joined[:, 128:]
    sig = 1.0 / (1.0 + jnp.exp(-gate))
    act = gate * sig
    grad_gate = grad * upper * sig * (1.0 + gate * (1.0 - sig))
    return (act * upper).astype(BF), grad_gate.astype(BF), (grad * act).astype(BF)


def dot(a, b, dims):
    return lax.dot_general(a, b, (dims, ((), ())), preferred_element_type=F32)


def tokens_kernel(me_ref, br_ref, tok_ref, w_ref, gh_ref, hid_ref, dx_ref, acc):
    step = pl.program_id(0)

    @pl.when(step == 0)
    def _():
        acc[...] = jnp.zeros_like(acc)

    group, half = step // 2, step % 2
    for jj in range(7):
        rows = [br_ref[group, k, half * 7 + jj] for k in range(4)]
        picked = jnp.concatenate([tok_ref[i] for i in rows], axis=1)
        wide = w_ref[0, :, jj].reshape(512, 256)
        joined = dot(picked, wide, ((1,), (0,)))
        span = slice(jj * 128, jj * 128 + 128)
        hidden, grad_gate, grad_up = swish_parts(joined, gh_ref[0, :, span].astype(F32))
        hid_ref[:, span] = hidden
        spread = dot(jnp.concatenate([grad_gate, grad_up], axis=1), wide, ((1,), (1,)))
        for k in range(4):
            acc[rows[k]] += spread[:, k * 128 : k * 128 + 128]

    @pl.when(step == pl.num_programs(0) - 1)
    def _():
        for b in range(64):
            dx_ref[:, b * 128 : b * 128 + 128] = acc[b].astype(BF)


def own_tokens(me, br, tok, wide, ghb):
    return pl.pallas_call(
        tokens_kernel,
        out_shape=(jax.ShapeDtypeStruct((128, 14336), BF), jax.ShapeDtypeStruct((128, 8192), BF)),
        grid_spec=pltpu.PrefetchScalarGridSpec(
            num_scalar_prefetch=2,
            grid=(16,),
            in_specs=[
                pl.BlockSpec((64, 128, 128), lambda s, me, br: (0, me[0], 0)),
                pl.BlockSpec((1, 4, 7, 128, 256), lambda s, me, br: (s // 2, 0, s % 2, 0, 0)),
                pl.BlockSpec((1, 128, 896), lambda s, me, br: (s // 2, 0, s % 2)),
            ],
            out_specs=(
                pl.BlockSpec((128, 896), lambda s, me, br: (0, s)),
                pl.BlockSpec((128, 8192), lambda s, me, br: (0, 0)),
            ),
            scratch_shapes=[pltpu.VMEM((64, 128, 128), F32)],
        ),
        compiler_params=pltpu.CompilerParams(vmem_limit_bytes=48 << 20),
        name="tokens",
    )(me, br, tok, wide, ghb)


def weights_kernel(me_ref, br_ref, tok_ref, w_ref, gh_ref, out_ref, grads):
    j = pl.program_id(0)
    rows = [br_ref[me_ref[0], k, j] for k in range(4)]
    wide = w_ref[0, :, 0].reshape(512, 256)
    for t in range(4):
        span = slice(t * 256, t * 256 + 256)
        picked = jnp.concatenate([tok_ref[i, span] for i in rows], axis=1)
        joined = dot(picked, wide, ((1,), (0,)))
        _, grad_gate, grad_up = swish_parts(joined, gh_ref[span].astype(F32))
        grads[span, :128] = grad_gate
        grads[span, 128:] = grad_up
    for k in range(4):
        out_ref[k, 0] = dot(tok_ref[rows[k]], grads[...], ((0,), (0,))).astype(BF)


def own_weights(me, br, tok, wide, grad_hidden):
    return pl.pallas_call(
        weights_kernel,
        out_shape=jax.ShapeDtypeStruct((4, 14, 128, 256), BF),
        grid_spec=pltpu.PrefetchScalarGridSpec(
            num_scalar_prefetch=2,
            grid=(14,),
            in_specs=[
                pl.BlockSpec(
                    (64, 1024, 128), lambda j, me, br: (0, 0, 0), pipeline_mode=pl.Buffered(1)
                ),
                pl.BlockSpec((1, 4, 1, 128, 256), lambda j, me, br: (me[0], 0, j, 0, 0)),
                pl.BlockSpec((1024, 128), lambda j, me, br: (0, j)),
            ],
            out_specs=pl.BlockSpec((4, 1, 128, 256), lambda j, me, br: (0, j, 0, 0)),
            scratch_shapes=[pltpu.VMEM((1024, 256), BF)],
        ),
        compiler_params=pltpu.CompilerParams(vmem_limit_bytes=48 << 20),
        name="weights",
    )(me, br, tok, wide, grad_hidden)


def reduce_part(go, dw, out, l0, l1, s0, s1, m0, m1, swap, x, z, y, core):
    e, zh = z % 2, z // 2
    first, started = [], []
    for d in range(1, 4):
        zd, xd = (z + d) % 4, (x + d) % 4
        first.append(go(dw.at[zd % 2, 0, :, :, zd // 2], l0.at[d - 1], at(x, zd, y, core)))
        first.append(go(dw.at[:, 1, :, xd], l1.at[d - 1], at(xd, z, y, core)))
    for c in first:
        c.wait_recv()

    def add0(j, _):
        total = dw[e, 0, j, :, zh].astype(F32)
        for d in range(3):
            total += l0[d, j].astype(F32)
        s0[j] = total.astype(BF)
        for ee in range(2):
            total = dw[ee, 1, j, x].astype(F32)
            for d in range(3):
                total += l1[d, ee, j].astype(F32)
            s1[ee, j] = total.astype(BF)
        return 0

    lax.fori_loop(0, 14, add0, 0)
    for d in range(1, 4):
        zd, xd = (z + d) % 4, (x + d) % 4
        started.append(go(s0.at[:, xd], m0.at[d - 1], at(xd, z, y, core)))
        started.append(go(s1.at[zd % 2, :, zd // 2], m1.at[d - 1], at(x, zd, y, core)))
    for c in started:
        c.wait_recv()
    for hf in range(2):
        total = (s0[:, x] if hf == 0 else s1[e, :, zh]).astype(F32)
        got = m0 if hf == 0 else m1
        for d in range(3):
            total += got[d].astype(F32)
        low, high = total[:, :8], total[:, 8:]
        mine = jnp.where(e == 0, low, high).astype(F32)
        other = jnp.where(e == 0, high, low).astype(F32)
        span = pl.ds(14 * hf, 14)
        out[e, span] = jnp.concatenate([mine[:, :, :128], mine[:, :, 128:]], axis=1).astype(BF)
        swap[span] = jnp.concatenate([other[:, :, :128], other[:, :, 128:]], axis=1).astype(BF)
    last = go(swap, out.at[e], at(x, z + 1 - 2 * e, y, core))
    last.wait()
    for c in first + started:
        c.wait_send()


REDUCE_SCRATCH = [
    pltpu.VMEM((3, 14, 4, 16, 256), BF),
    pltpu.VMEM((3, 2, 14, 2, 16, 256), BF),
    pltpu.VMEM((14, 4, 16, 256), BF),
    pltpu.VMEM((2, 14, 2, 16, 256), BF),
    pltpu.VMEM((3, 14, 16, 256), BF),
    pltpu.VMEM((3, 14, 16, 256), BF),
    pltpu.VMEM((28, 16, 128), BF),
]


def reduce_kernel(dw, out, l0, l1, s0, s1, m0, m1, swap, send, recv):
    x, z, y, core = place()
    greet([at((x + d) % 4, z, y, core) for d in range(1, 4)] + [at(x, (z + d) % 4, y, core) for d in range(1, 4)])
    reduce_part(Wires(send, recv).copy, dw, out, l0, l1, s0, s1, m0, m1, swap, x, z, y, core)


def reduce_weights(dw):
    return pl.pallas_call(
        reduce_kernel,
        out_shape=jax.ShapeDtypeStruct((2, 28, 16, 128), BF),
        in_specs=[VMEM],
        out_specs=VMEM,
        scratch_shapes=REDUCE_SCRATCH
        + [pltpu.SemaphoreType.DMA((13,)), pltpu.SemaphoreType.DMA((13,))],
        compiler_params=pltpu.CompilerParams(
            collective_id=2, has_side_effects=True, vmem_limit_bytes=32 << 20
        ),
        name="reduce",
    )(dw)


def shards(tokens, weights, block_rows, grad_hidden):
    wv, brp = views(weights, block_rows)
    tok, wide, ghb, br = gather_all(tokens, wv, grad_hidden, brp)
    tok = tok.reshape(64, 1024, 128)
    wide = wide.reshape(8, 4, 14, 128, 256)
    me = lax.axis_index("col").astype(jnp.int32).reshape(1)
    dw = own_weights(me, br, tok, wide, grad_hidden)
    out = reduce_weights(dw.reshape(2, 2, 14, 4, 2, 16, 256))
    grad_w = out.reshape(4, 14, 2, 8, 128).transpose(0, 1, 3, 2, 4).reshape(4, 14, 8, 256)
    hidden, grad_tok = own_tokens(me, br, tok, wide, ghb)
    return hidden, grad_tok, grad_w


def solution(mesh):
    return jax.shard_map(
        shards,
        mesh=mesh,
        in_specs=(P("row", "col"), P(None, "col", "row", None), P(None, "col"), P("row", "col")),
        out_specs=(P(("row", "col"), None), P(("row", "col"), None), P(None, "col", "row", None)),
        check_vma=False,
    )
```

```python
import jax
import jax.numpy as jnp
from jax import lax
from jax.experimental import pallas as pl
from jax.experimental.pallas import tpu as pltpu
from jax.sharding import PartitionSpec as P

MESH = pl.DeviceIdType.MESH
BF, F32 = jnp.bfloat16, jnp.float32
ANY = pl.BlockSpec(memory_space=pl.ANY)
WIRES = 106
VMEM = pl.BlockSpec(memory_space=pltpu.VMEM)


def place():
    row, col = lax.axis_index("row"), lax.axis_index("col")
    return row // 4, row % 4, col // 2, col % 2


def at(x, z, y, core):
    return (x * 4 + z, y * 2 + core)


def greet(peers):
    barrier = pltpu.get_barrier_semaphore()
    for peer in peers:
        pl.semaphore_signal(barrier, inc=1, device_id=peer, device_id_type=MESH)
    pl.semaphore_wait(barrier, len(peers))


class Wires:
    def __init__(self, send, recv):
        self.send, self.recv, self.made = send, recv, 0
        self.unsent, self.ungot = [], []

    def copy(self, src, dst, peer):
        i = self.made
        self.made += 1
        c = pltpu.make_async_remote_copy(
            src_ref=src,
            dst_ref=dst,
            send_sem=self.send.at[i],
            recv_sem=self.recv.at[i],
            device_id=peer,
            device_id_type=MESH,
        )
        c.start()
        self.unsent.append(c)
        self.ungot.append(c)
        return c

    def sent(self, *copies):
        for c in copies:
            self.unsent = [o for o in self.unsent if o is not c]
            c.wait_send()

    def got(self, *copies):
        for c in copies:
            self.ungot = [o for o in self.ungot if o is not c]
            c.wait_recv()

    def finish(self):
        self.got(*list(self.ungot))
        self.sent(*list(self.unsent))


def weight_terms(half, br_ref, tok, own_w, gh, grads, acc, dw):
    def column(j, _):
        rows = [br_ref[k, j] for k in range(4)]
        wide = jnp.concatenate(
            [own_w[k // 2, k % 2, j].reshape(128, 256) for k in range(4)], axis=0
        )
        lane = pl.ds(pl.multiple_of(j * 128, 128), 128)
        for t in range(2):
            span = slice(t * 256, t * 256 + 256)
            picked = jnp.concatenate([tok[i, span] for i in rows], axis=1)
            joined = dot(picked, wide, ((1,), (0,)))
            grad = gh[pl.ds(half * 512 + t * 256, 256), lane].astype(F32)
            _, grad_gate, grad_up = swish_parts(joined, grad)
            grads[span, :128] = grad_gate
            grads[span, 128:] = grad_up
        for k in range(4):
            term = dot(tok[rows[k]], grads[...], ((0,), (0,)))
            if half == 0:
                acc[k, j] = term
            else:
                total = (acc[k, j] + term).astype(BF)
                dw[k // 2, k % 2, j] = total.reshape(4, 2, 16, 256)
        return 0

    lax.fori_loop(0, 14, column, 0)


def gather_kernel(
    tok_ref, wv_ref, gh_ref, br_ref, rows_ref,
    tokown, wide, ghb, brb, out,
    tok0, tok1, wp, slab, own_w, gh, grads, acc, dw,
    l0, l1, s0, s1, m0, m1, swap,
    send, recv, local,
):
    x, z, y, core = place()
    col = y * 2 + core
    e, zh = z % 2, z // 2
    yp, ym, y2 = (y + 1) % 4, (y + 3) % 4, (y + 2) % 4
    zp, zm, z2 = (z + 1) % 4, (z + 3) % 4, (z + 2) % 4
    xp, xm, x2 = (x + 1) % 4, (x + 3) % 4, (x + 2) % 4
    sib = at(x, z, y, 1 - core)
    cols = [(col + d) % 8 for d in range(1, 8)]
    col_peers = [at(x, z, c // 2, c % 2) for c in cols]
    x_peers = [at(v, z, y, core) for v in (xp, xm, x2)]
    z_peers = [at(x, v, y, core) for v in (zp, zm, z2)]
    greet(col_peers + x_peers + z_peers)
    wires = Wires(send, recv)
    go, sent, got = wires.copy, wires.sent, wires.got
    locals_made = [0]

    def lcopy(src, dst):
        c = pltpu.make_async_copy(src, dst, local.at[locals_made[0]])
        locals_made[0] += 1
        c.start()
        return c

    pair = go(wv_ref.at[1 - e], wp, at(x, z + 1 - 2 * e, y, core))
    base = col * 8
    toks = (tok0, tok1)
    own_tok = [
        lcopy(tok_ref.at[pl.ds(512 * r, 512), pl.ds(m * 128, 128)], toks[r].at[base + m])
        for r in range(2)
        for m in range(8)
    ]
    for c, p in zip(cols, col_peers):
        go(br_ref, brb.at[col], p)
    own_br = lcopy(br_ref, brb.at[col])
    own_gh = lcopy(gh_ref, gh)
    own_ghb = lcopy(gh_ref.at[pl.ds(pl.multiple_of(col * 128, 128), 128)], ghb.at[col])

    got(pair)
    mine, other = wv_ref[e].astype(F32), wp[...].astype(F32)
    low = jnp.where(e == 0, mine, other)
    high = jnp.where(e == 0, other, mine)
    gate = jnp.concatenate([low[:, :8], high[:, :8]], axis=1).astype(BF)
    upper = jnp.concatenate([low[:, 8:], high[:, 8:]], axis=1).astype(BF)
    slab[:, :, :, :128] = gate.reshape(2, 14, 16, 128)
    slab[:, :, :, 128:] = upper.reshape(2, 14, 16, 128)
    placed = lcopy(slab, wide.at[0, core, e, :, :, x, zh])
    early = [go(slab.at[0], wide.at[0, core, e, 0, :, x, zh], p) for p in x_peers]
    early += [go(slab.at[1], wide.at[0, core, e, 1, :, x, zh], p) for p in z_peers]
    ystage = [
        go(slab, wide.at[(y + 4 - v) % 4, core, e, :, :, x, zh], at(x, z, v, core))
        for v in (yp, ym, y2)
    ]
    for c in own_tok:
        c.wait()
    up, down = at(x, z, yp, core), at(x, z, ym, core)

    def tsend(r, yy, h, peer):
        part = toks[r].at[pl.ds((yy * 2 + core) * 8 + 4 * h, 4)]
        return go(part, part, peer)

    sib_tok = [[], []]

    def tshare(r, *parts):
        for yy, h in parts:
            sib_tok[r].append(tsend(r, yy, h, sib))

    def same(part, peer):
        return go(part, part, peer)

    ta_up, tb_dn = tsend(0, y, 0, up), tsend(0, y, 1, down)
    tshare(0, (y, 0), (y, 1))
    tshare(1, (y, 0), (y, 1))

    placed.wait()
    got(*early)
    second = [same(wide.at[0, core, e, 0, :, :, zh], p) for p in z_peers]
    second += [same(wide.at[0, core, :, 1, :, x], p) for p in x_peers]
    got(*ystage)
    others = pl.ds(1, 3)
    first = [same(wide.at[others, core, e, 0, :, x, zh], p) for p in x_peers]
    first += [same(wide.at[others, core, e, 1, :, x, zh], p) for p in z_peers]

    sent(ta_up, tb_dn)
    got(ta_up, tb_dn)
    tb_up, ta_dn = tsend(0, y, 1, up), tsend(0, y, 0, down)
    ta_fwd, tb_fwd = tsend(0, ym, 0, up), tsend(0, yp, 1, down)
    tshare(0, (ym, 0), (yp, 1))

    got(*second)
    own_copy = lcopy(wide.at[0, core], own_w)
    got(*first)

    def w0(zz, h):
        return wide.at[others, core, zz % 2, 0, pl.ds(7 * h, 7), :, zz // 2]

    def w1(xx, h):
        return wide.at[others, core, :, 1, pl.ds(7 * h, 7), xx]

    zup, zdn = at(x, zp, y, core), at(x, zm, y, core)
    xup, xdn = at(xp, z, y, core), at(xm, z, y, core)
    a0u, b0d = same(w0(z, 0), zup), same(w0(z, 1), zdn)
    a1u, b1d = same(w1(x, 0), xup), same(w1(x, 1), xdn)
    own_copy.wait()
    same(wide.at[0, core], sib)
    for h in range(2):
        same(w0(z, h), sib)
        same(w1(x, h), sib)

    got(tb_up, ta_dn, ta_fwd, tb_fwd)
    tshare(0, (ym, 1), (yp, 0), (y2, 0), (y2, 1))
    sent(tb_up, ta_dn, ta_fwd, tb_fwd)
    ta_up, tb_dn = tsend(1, y, 0, up), tsend(1, y, 1, down)
    own_gh.wait()
    got(*sib_tok[0])
    weight_terms(0, rows_ref, tok0, own_w, gh, grads, acc, dw)

    sent(ta_up, tb_dn)
    got(ta_up, tb_dn)
    tb_up, ta_dn = tsend(1, y, 1, up), tsend(1, y, 0, down)
    ta_fwd, tb_fwd = tsend(1, ym, 0, up), tsend(1, yp, 1, down)
    tshare(1, (ym, 0), (yp, 1))

    got(a0u, b0d, a1u, b1d)
    b0u, a0d = same(w0(z, 1), zup), same(w0(z, 0), zdn)
    b1u, a1d = same(w1(x, 1), xup), same(w1(x, 0), xdn)
    a0f, b0f = same(w0(zm, 0), zup), same(w0(zp, 1), zdn)
    a1f, b1f = same(w1(xm, 0), xup), same(w1(xp, 1), xdn)
    for part in (w0(zm, 0), w0(zp, 1), w1(xm, 0), w1(xp, 1)):
        same(part, sib)

    got(tb_up, ta_dn, ta_fwd, tb_fwd)
    tshare(1, (ym, 1), (yp, 0), (y2, 0), (y2, 1))
    sent(tb_up, ta_dn, ta_fwd, tb_fwd)
    for c, p in zip(cols, col_peers):
        go(gh_ref.at[pl.ds(pl.multiple_of(c * 128, 128), 128)], ghb.at[col], p)
    got(*sib_tok[1])
    rows_at = pl.ds(pl.multiple_of(col % 4 * 128, 128), 128)
    keep = [pltpu.make_async_copy(t.at[:, rows_at], tokown, local.at[21]) for t in toks]
    for h in range(2):
        pl.when(col // 4 == h)(keep[h].start)
    weight_terms(1, rows_ref, tok1, own_w, gh, grads, acc, dw)

    got(b0u, a0d, b1u, a1d, a0f, b0f, a1f, b1f)
    for part in (w0(zm, 1), w0(zp, 0), w1(xm, 1), w1(xp, 0)):
        same(part, sib)
    for h in range(2):
        same(w0(z2, h), sib)
        same(w1(x2, h), sib)
    reduce_part(wires, dw, out, l0, l1, s0, s1, m0, m1, swap, x, z, y, core)
    for c in (own_br, own_ghb, keep[0]):
        c.wait()
    wires.finish()


def gather_all(tokens, wv, grad_hidden, br):
    return pl.pallas_call(
        gather_kernel,
        out_shape=(
            jax.ShapeDtypeStruct((64, 128, 128), BF),
            jax.ShapeDtypeStruct((4, 2, 2, 2, 14, 4, 2, 16, 256), BF),
            jax.ShapeDtypeStruct((8, 128, 1792), BF),
            jax.ShapeDtypeStruct((8, 8, 128), jnp.int32),
            jax.ShapeDtypeStruct((2, 28, 16, 128), BF),
        ),
        in_specs=[ANY, VMEM, ANY, ANY, pl.BlockSpec(memory_space=pltpu.SMEM)],
        out_specs=(ANY, ANY, ANY, ANY, VMEM),
        scratch_shapes=[
            pltpu.VMEM((64, 512, 128), BF),
            pltpu.VMEM((64, 512, 128), BF),
            pltpu.VMEM((28, 16, 128), BF),
            pltpu.VMEM((2, 14, 16, 256), BF),
            pltpu.VMEM((2, 2, 14, 4, 2, 16, 256), BF),
            pltpu.VMEM((1024, 1792), BF),
            pltpu.VMEM((512, 256), BF),
            pltpu.VMEM((4, 14, 128, 256), F32),
            pltpu.VMEM((2, 2, 14, 4, 2, 16, 256), BF),
        ]
        + REDUCE_SCRATCH
        + [
            pltpu.SemaphoreType.DMA((WIRES,)),
            pltpu.SemaphoreType.DMA((WIRES,)),
            pltpu.SemaphoreType.DMA((22,)),
        ],
        compiler_params=pltpu.CompilerParams(
            collective_id=1, has_side_effects=True, vmem_limit_bytes=60 << 20
        ),
        name="gather",
    )(tokens, wv, grad_hidden, br, br)


def views(weights, block_rows):
    wv = weights.reshape(4, 14, 8, 2, 128).transpose(0, 1, 3, 2, 4).reshape(2, 28, 16, 128)
    br = jnp.pad(block_rows, ((0, 4), (0, 114)))
    return wv, br


def swish_parts(joined, grad):
    gate, upper = joined[:, :128], joined[:, 128:]
    sig = 1.0 / (1.0 + jnp.exp(-gate))
    act = gate * sig
    grad_gate = grad * upper * sig * (1.0 + gate * (1.0 - sig))
    return (act * upper).astype(BF), grad_gate.astype(BF), (grad * act).astype(BF)


def dot(a, b, dims):
    return lax.dot_general(a, b, (dims, ((), ())), preferred_element_type=F32)


def tokens_kernel(me_ref, br_ref, tok_ref, w_ref, gh_ref, hid_ref, dx_ref, acc):
    step = pl.program_id(0)

    @pl.when(step == 0)
    def _():
        acc[...] = jnp.zeros_like(acc)

    group, half = step // 2, step % 2
    for jj in range(7):
        rows = [br_ref[group, k, half * 7 + jj] for k in range(4)]
        picked = jnp.concatenate([tok_ref[i] for i in rows], axis=1)
        wide = w_ref[0, :, jj].reshape(512, 256)
        joined = dot(picked, wide, ((1,), (0,)))
        span = slice(jj * 128, jj * 128 + 128)
        hidden, grad_gate, grad_up = swish_parts(joined, gh_ref[0, :, span].astype(F32))
        hid_ref[:, span] = hidden
        spread = dot(jnp.concatenate([grad_gate, grad_up], axis=1), wide, ((1,), (1,)))
        for k in range(4):
            acc[rows[k]] += spread[:, k * 128 : k * 128 + 128]

    @pl.when(step == pl.num_programs(0) - 1)
    def _():
        for b in range(64):
            dx_ref[:, b * 128 : b * 128 + 128] = acc[b].astype(BF)


def relative(s, me, br):
    group = s // 2
    away = lax.rem(group // 2 - me[0] // 2 + 4, 4)
    return (away * 2 + group % 2, 0, s % 2, 0, 0)


def own_tokens(me, br, tok, wide, ghb):
    return pl.pallas_call(
        tokens_kernel,
        out_shape=(jax.ShapeDtypeStruct((128, 14336), BF), jax.ShapeDtypeStruct((128, 8192), BF)),
        grid_spec=pltpu.PrefetchScalarGridSpec(
            num_scalar_prefetch=2,
            grid=(16,),
            in_specs=[
                pl.BlockSpec((64, 128, 128), lambda s, me, br: (0, 0, 0)),
                pl.BlockSpec((1, 4, 7, 128, 256), relative),
                pl.BlockSpec((1, 128, 896), lambda s, me, br: (s // 2, 0, s % 2)),
            ],
            out_specs=(
                pl.BlockSpec((128, 896), lambda s, me, br: (0, s)),
                pl.BlockSpec((128, 8192), lambda s, me, br: (0, 0)),
            ),
            scratch_shapes=[pltpu.VMEM((64, 128, 128), F32)],
        ),
        compiler_params=pltpu.CompilerParams(vmem_limit_bytes=48 << 20),
        name="tokens",
    )(me, br, tok, wide, ghb)


def reduce_part(wires, dw, out, l0, l1, s0, s1, m0, m1, swap, x, z, y, core):
    go = wires.copy
    e, zh = z % 2, z // 2
    first, started = [], []
    for d in range(1, 4):
        zd, xd = (z + d) % 4, (x + d) % 4
        first.append(go(dw.at[zd % 2, 0, :, :, zd // 2], l0.at[d - 1], at(x, zd, y, core)))
        first.append(go(dw.at[:, 1, :, xd], l1.at[d - 1], at(xd, z, y, core)))
    wires.got(*first)

    def add0(j, _):
        total = dw[e, 0, j, :, zh].astype(F32)
        for d in range(3):
            total += l0[d, j].astype(F32)
        s0[j] = total.astype(BF)
        for ee in range(2):
            total = dw[ee, 1, j, x].astype(F32)
            for d in range(3):
                total += l1[d, ee, j].astype(F32)
            s1[ee, j] = total.astype(BF)
        return 0

    lax.fori_loop(0, 14, add0, 0)
    for d in range(1, 4):
        zd, xd = (z + d) % 4, (x + d) % 4
        started.append(go(s0.at[:, xd], m0.at[d - 1], at(xd, z, y, core)))
        started.append(go(s1.at[zd % 2, :, zd // 2], m1.at[d - 1], at(x, zd, y, core)))
    wires.got(*started)
    for hf in range(2):
        total = (s0[:, x] if hf == 0 else s1[e, :, zh]).astype(F32)
        got = m0 if hf == 0 else m1
        for d in range(3):
            total += got[d].astype(F32)
        low, high = total[:, :8], total[:, 8:]
        mine = jnp.where(e == 0, low, high).astype(F32)
        other = jnp.where(e == 0, high, low).astype(F32)
        span = pl.ds(14 * hf, 14)
        out[e, span] = jnp.concatenate([mine[:, :, :128], mine[:, :, 128:]], axis=1).astype(BF)
        swap[span] = jnp.concatenate([other[:, :, :128], other[:, :, 128:]], axis=1).astype(BF)
    go(swap, out.at[e], at(x, z + 1 - 2 * e, y, core))


REDUCE_SCRATCH = [
    pltpu.VMEM((3, 14, 4, 16, 256), BF),
    pltpu.VMEM((3, 2, 14, 2, 16, 256), BF),
    pltpu.VMEM((14, 4, 16, 256), BF),
    pltpu.VMEM((2, 14, 2, 16, 256), BF),
    pltpu.VMEM((3, 14, 16, 256), BF),
    pltpu.VMEM((3, 14, 16, 256), BF),
    pltpu.VMEM((28, 16, 128), BF),
]


def shards(tokens, weights, block_rows, grad_hidden):
    wv, brp = views(weights, block_rows)
    tok, wide, ghb, br, out = gather_all(tokens, wv, grad_hidden, brp)
    wide = wide.reshape(8, 4, 14, 128, 256)
    me = lax.axis_index("col").astype(jnp.int32).reshape(1)
    grad_w = out.reshape(4, 14, 2, 8, 128).transpose(0, 1, 3, 2, 4).reshape(4, 14, 8, 256)
    hidden, grad_tok = own_tokens(me, br, tok, wide, ghb)
    return hidden, grad_tok, grad_w


def solution(mesh):
    return jax.shard_map(
        shards,
        mesh=mesh,
        in_specs=(P("row", "col"), P(None, "col", "row", None), P(None, "col"), P("row", "col")),
        out_specs=(P(("row", "col"), None), P(("row", "col"), None), P(None, "col", "row", None)),
        check_vma=False,
    )
```

```python
import jax
import jax.numpy as jnp
from jax import lax
from jax.experimental import pallas as pl
from jax.experimental.pallas import tpu as pltpu
from jax.sharding import PartitionSpec as P

MESH = pl.DeviceIdType.MESH
BF, F32 = jnp.bfloat16, jnp.float32
HBM = pl.BlockSpec(memory_space=pltpu.HBM)
WIRES, LOCALS = 88, 24
VMEM = pl.BlockSpec(memory_space=pltpu.VMEM)


def place():
    row, col = lax.axis_index("row"), lax.axis_index("col")
    return row // 4, row % 4, col // 2, col % 2


def at(x, z, y, core):
    return (x * 4 + z, y * 2 + core)


def greet(peers):
    barrier = pltpu.get_barrier_semaphore()
    for peer in peers:
        pl.semaphore_signal(barrier, inc=1, device_id=peer, device_id_type=MESH)
    pl.semaphore_wait(barrier, len(peers))


class Wires:
    def __init__(self, send, recv):
        self.send, self.recv, self.made = send, recv, 0
        self.unsent, self.ungot = [], []

    def copy(self, src, dst, peer):
        i = self.made
        self.made += 1
        c = pltpu.make_async_remote_copy(
            src_ref=src,
            dst_ref=dst,
            send_sem=self.send.at[i],
            recv_sem=self.recv.at[i],
            device_id=peer,
            device_id_type=MESH,
        )
        c.start()
        self.unsent.append(c)
        self.ungot.append(c)
        return c

    def sent(self, *copies):
        for c in copies:
            self.unsent = [o for o in self.unsent if o is not c]
            c.wait_send()

    def got(self, *copies):
        for c in copies:
            self.ungot = [o for o in self.ungot if o is not c]
            c.wait_recv()

    def finish(self):
        self.got(*list(self.ungot))
        self.sent(*list(self.unsent))


def weight_terms(half, columns, br_ref, tok, own_w, gh, picked, grads, acc, dw):
    def column(j, _):
        rows = [br_ref[k, j] for k in range(4)]
        wide = jnp.concatenate(
            [own_w[k // 2, k % 2, j].reshape(128, 256) for k in range(4)], axis=0
        )
        lane = pl.ds(pl.multiple_of(j * 128, 128), 128)
        for k in range(4):
            picked[:, k * 128 : k * 128 + 128] = tok[rows[k]]
        for t in range(2):
            span = slice(t * 256, t * 256 + 256)
            joined = dot(picked[span], wide, ((1,), (0,)))
            grad = gh[pl.ds(half * 512 + t * 256, 256), lane].astype(F32)
            _, grad_gate, grad_up = swish_parts(joined, grad)
            grads[span, :128] = grad_gate
            grads[span, 128:] = grad_up
        term = dot(picked[...], grads[...], ((0,), (0,)))
        if half == 0:
            acc[j] = term
        else:
            total = (acc[j] + term).astype(BF).reshape(4, 4, 2, 16, 256)
            for k in range(4):
                dw[k // 2, k % 2, j] = total[k]
        return 0

    lax.fori_loop(columns[0], columns[1], column, 0)


def gather_kernel(
    tok_ref, wv_ref, gh_ref, br_ref, rows_ref,
    tokb, wide, ghb, brb, out,
    tok, tokv, wv, wp, slab, own_w, gh, picked, grads, acc, dw,
    l0, l1, s0, s1, m0, m1, swap,
    send, recv, local,
):
    x, z, y, core = place()
    col = y * 2 + core
    e, zh = z % 2, z // 2
    yp, ym, y2 = (y + 1) % 4, (y + 3) % 4, (y + 2) % 4
    zp, zm, z2 = (z + 1) % 4, (z + 3) % 4, (z + 2) % 4
    xp, xm, x2 = (x + 1) % 4, (x + 3) % 4, (x + 2) % 4
    sib = at(x, z, y, 1 - core)
    up, down = at(x, z, yp, core), at(x, z, ym, core)
    cols = [(col + d) % 8 for d in range(1, 8)]
    col_peers = [at(x, z, c // 2, c % 2) for c in cols]
    x_peers = [at(v, z, y, core) for v in (xp, xm, x2)]
    z_peers = [at(x, v, y, core) for v in (zp, zm, z2)]
    wires = Wires(send, recv)
    go, sent, got = wires.copy, wires.sent, wires.got
    locals_made = [0]

    def lcopy(src, dst):
        c = pltpu.make_async_copy(src, dst, local.at[locals_made[0]])
        locals_made[0] += 1
        c.start()
        return c

    def same(part, peer):
        return go(part, part, peer)

    staged = lcopy(tok_ref, tokv)
    own_wv = lcopy(wv_ref.at[e], wv)
    staged.wait()
    own_tok = [
        [
            lcopy(
                tokv.at[pl.ds(512 * r, 512), pl.ds(m * 128, 128)], tok[r].at[col * 8 + m]
            )
            for m in range(8)
        ]
        for r in range(2)
    ]
    own_br = lcopy(br_ref, brb.at[col])
    own_gh = lcopy(gh_ref, gh)
    own_ghb = lcopy(gh_ref.at[pl.ds(pl.multiple_of(col * 128, 128), 128)], ghb.at[col])
    greet(col_peers + x_peers + z_peers)
    pair = go(wv_ref.at[1 - e], wp, at(x, z + 1 - 2 * e, y, core))

    def shard(r, yy, cc):
        return tok[r].at[pl.ds((yy * 2 + cc) * 8, 8)]

    def half_shard(r, yy, h):
        return tok[r].at[pl.ds((yy * 2 + core) * 8 + 4 * h, 4)]

    def start_tokens(r):
        sends = [same(shard(r, y, core), p) for p in (up, down)]
        return sends, [same(shard(r, y, core), sib)]

    def forward_tokens(r, sends, shares):
        got(*sends)
        shares += [same(shard(r, v, core), sib) for v in (ym, yp)]
        return [same(half_shard(r, ym, 0), up), same(half_shard(r, yp, 1), down)]

    def finish_tokens(r, shares, forwards):
        got(*shares)
        got(*forwards)
        got(same(shard(r, y2, core), sib))

    for c in own_tok[0]:
        c.wait()
    sends0, shares0 = start_tokens(0)
    for c, p in zip(cols, col_peers):
        go(br_ref, brb.at[col], p)
    own_wv.wait()
    got(pair)
    mine, other = wv[...].astype(F32), wp[...].astype(F32)
    low = jnp.where(e == 0, mine, other)
    high = jnp.where(e == 0, other, mine)
    gate = jnp.concatenate([low[:, :8], high[:, :8]], axis=1).astype(BF)
    upper = jnp.concatenate([low[:, 8:], high[:, 8:]], axis=1).astype(BF)
    slab[:, :, :, :128] = gate.reshape(2, 14, 16, 128)
    slab[:, :, :, 128:] = upper.reshape(2, 14, 16, 128)
    ystage = [
        go(slab, wide.at[(y + 4 - v) % 4, core, e, :, :, x, zh], at(x, z, v, core))
        for v in (yp, ym, y2)
    ]
    placed = lcopy(slab, wide.at[0, core, e, :, :, x, zh])
    early = [go(slab.at[0], wide.at[0, core, e, 0, :, x, zh], p) for p in x_peers]
    early += [go(slab.at[1], wide.at[0, core, e, 1, :, x, zh], p) for p in z_peers]
    placed.wait()
    got(*early)
    second = [same(wide.at[0, core, e, 0, :, :, zh], p) for p in z_peers]
    second += [same(wide.at[0, core, :, 1, :, x], p) for p in x_peers]
    got(*ystage)
    others = pl.ds(1, 3)
    first = [same(wide.at[others, core, e, 0, :, x, zh], p) for p in x_peers]
    first += [same(wide.at[others, core, e, 1, :, x, zh], p) for p in z_peers]

    for c in own_tok[1]:
        c.wait()
    forwards0 = forward_tokens(0, sends0, shares0)
    sends1, shares1 = start_tokens(1)
    got(*second)
    own_copy = lcopy(wide.at[0, core], own_w)
    got(*first)

    def w0(zz, js):
        return wide.at[others, core, zz % 2, 0, js, :, zz // 2]

    def w1(xx, js):
        return wide.at[others, core, :, 1, js, xx]

    every, lower, higher = pl.ds(0, 14), pl.ds(0, 7), pl.ds(7, 7)
    zup, zdn = at(x, zp, y, core), at(x, zm, y, core)
    xup, xdn = at(xp, z, y, core), at(xm, z, y, core)
    third = [same(w0(z, every), p) for p in (zup, zdn)] + [same(w1(x, every), p) for p in (xup, xdn)]
    for part in (w0(z, every), w1(x, every)):
        same(part, sib)
    own_copy.wait()
    same(wide.at[0, core], sib)

    finish_tokens(0, shares0, forwards0)
    own_gh.wait()
    terms = (rows_ref, tok[0], own_w, gh, picked, grads, acc, dw)
    weight_terms(0, (0, 14), *terms)

    forwards1 = forward_tokens(1, sends1, shares1)
    got(*third)
    fourth = [same(w0(zm, lower), zup), same(w0(zp, higher), zdn)]
    fourth += [same(w1(xm, lower), xup), same(w1(xp, higher), xdn)]
    for part in (w0(zm, every), w0(zp, every), w1(xm, every), w1(xp, every)):
        same(part, sib)

    finish_tokens(1, shares1, forwards1)
    sent(*forwards1)
    for c, p in zip(cols, col_peers):
        go(gh_ref.at[pl.ds(pl.multiple_of(c * 128, 128), 128)], ghb.at[col], p)
    rows_at = pl.ds(pl.multiple_of(col % 4 * 128, 128), 128)
    keep = [pltpu.make_async_copy(t.at[:, rows_at], tokb, local.at[LOCALS - 1]) for t in tok]
    for h in range(2):
        pl.when(col // 4 == h)(keep[h].start)
    terms = (rows_ref, tok[1], own_w, gh, picked, grads, acc, dw)
    summing = []
    for js in ((0, 7), (7, 14)):
        weight_terms(1, js, *terms)
        summing += reduce_start(wires, js, dw, l0, l1, x, z, y, core)

    got(*fourth)
    for part in (w0(z2, every), w1(x2, every)):
        same(part, sib)
    reduce_part(wires, summing, dw, out, l0, l1, s0, s1, m0, m1, swap, x, z, y, core)
    own_br.wait()
    own_ghb.wait()
    keep[0].wait()
    wires.finish()
    assert (wires.made, locals_made[0]) == (WIRES, LOCALS - 1), (wires.made, locals_made[0])


def gather_all(tokens, wv, grad_hidden, br):
    return pl.pallas_call(
        gather_body,
        out_shape=(
            jax.ShapeDtypeStruct((64, 128, 128), BF),
            jax.ShapeDtypeStruct((4, 2, 2, 2, 14, 4, 2, 16, 256), BF),
            jax.ShapeDtypeStruct((8, 128, 1792), BF),
            jax.ShapeDtypeStruct((8, 4, 14), jnp.int32),
            jax.ShapeDtypeStruct((2, 28, 16, 128), BF),
        ),
        in_specs=[HBM, HBM, HBM, HBM, pl.BlockSpec(memory_space=pltpu.SMEM)],
        out_specs=(HBM, HBM, HBM, HBM, VMEM),
        scratch_shapes=[
            pltpu.VMEM((64, 512, 128), BF),
            pltpu.VMEM((64, 512, 128), BF),
            pltpu.VMEM((1024, 1024), BF),
            pltpu.VMEM((28, 16, 128), BF),
            pltpu.VMEM((28, 16, 128), BF),
            pltpu.VMEM((2, 14, 16, 256), BF),
            pltpu.VMEM((2, 2, 14, 4, 2, 16, 256), BF),
            pltpu.VMEM((1024, 1792), BF),
            pltpu.VMEM((512, 512), BF),
            pltpu.VMEM((512, 256), BF),
            pltpu.VMEM((14, 512, 256), F32),
            pltpu.VMEM((2, 2, 14, 4, 2, 16, 256), BF),
        ]
        + REDUCE_SCRATCH
        + [
            pltpu.SemaphoreType.DMA((WIRES,)),
            pltpu.SemaphoreType.DMA((WIRES,)),
            pltpu.SemaphoreType.DMA((LOCALS,)),
        ],
        compiler_params=pltpu.CompilerParams(
            collective_id=1, has_side_effects=True, vmem_limit_bytes=60 << 20
        ),
        name="gather",
    )(tokens, wv, grad_hidden, br, br)


def gather_body(*refs):
    gather_kernel(*refs[:10], refs[10:12], *refs[12:])


def views(weights, block_rows):
    wv = weights.reshape(4, 14, 8, 2, 128).transpose(0, 1, 3, 2, 4).reshape(2, 28, 16, 128)
    return wv, block_rows


def swish_parts(joined, grad):
    gate, upper = joined[:, :128], joined[:, 128:]
    sig = 1.0 / (1.0 + jnp.exp(-gate))
    act = gate * sig
    grad_gate = grad * upper * sig * (1.0 + gate * (1.0 - sig))
    return (act * upper).astype(BF), grad_gate.astype(BF), (grad * act).astype(BF)


def dot(a, b, dims):
    return lax.dot_general(a, b, (dims, ((), ())), preferred_element_type=F32)


def tokens_kernel(me_ref, br_ref, tok_ref, w_ref, gh_ref, hid_ref, dx_ref, acc, grads):
    step = pl.program_id(0)

    @pl.when(step == 0)
    def _():
        acc[...] = jnp.zeros_like(acc)

    rows = [[br_ref[step, k, j] for k in range(4)] for j in range(14)]
    for j in range(14):
        picked = jnp.concatenate([tok_ref[i] for i in rows[j]], axis=1)
        joined = dot(picked, w_ref[0, :, j].reshape(512, 256), ((1,), (0,)))
        span = slice(j * 128, j * 128 + 128)
        hidden, grad_gate, grad_up = swish_parts(joined, gh_ref[0, :, span].astype(F32))
        hid_ref[:, span] = hidden
        grads[j, :, :128] = grad_gate
        grads[j, :, 128:] = grad_up
    for j in range(14):
        spread = dot(grads[j], w_ref[0, :, j].reshape(512, 256), ((1,), (1,)))
        for k in range(4):
            acc[rows[j][k]] += spread[:, k * 128 : k * 128 + 128]

    @pl.when(step == pl.num_programs(0) - 1)
    def _():
        for b in range(64):
            dx_ref[:, b * 128 : b * 128 + 128] = acc[b].astype(BF)


def relative(s, me, br):
    away = lax.rem(s // 2 - me[0] // 2 + 4, 4)
    return (away * 2 + s % 2, 0, 0, 0, 0)


def own_tokens(me, br, tok, wide, ghb):
    return pl.pallas_call(
        tokens_kernel,
        out_shape=(jax.ShapeDtypeStruct((128, 14336), BF), jax.ShapeDtypeStruct((128, 8192), BF)),
        grid_spec=pltpu.PrefetchScalarGridSpec(
            num_scalar_prefetch=2,
            grid=(8,),
            in_specs=[
                pl.BlockSpec((64, 128, 128), lambda s, me, br: (0, 0, 0)),
                pl.BlockSpec((1, 4, 14, 128, 256), relative),
                pl.BlockSpec((1, 128, 1792), lambda s, me, br: (s, 0, 0)),
            ],
            out_specs=(
                pl.BlockSpec((128, 1792), lambda s, me, br: (0, s)),
                pl.BlockSpec((128, 8192), lambda s, me, br: (0, 0)),
            ),
            scratch_shapes=[pltpu.VMEM((64, 128, 128), F32), pltpu.VMEM((14, 128, 256), BF)],
        ),
        compiler_params=pltpu.CompilerParams(vmem_limit_bytes=48 << 20),
        name="tokens",
    )(me, br, tok, wide, ghb)


def reduce_start(wires, columns, dw, l0, l1, x, z, y, core):
    js, made = pl.ds(columns[0], columns[1] - columns[0]), []
    for d in range(1, 4):
        zd, xd = (z + d) % 4, (x + d) % 4
        made.append(
            wires.copy(dw.at[zd % 2, 0, js, :, zd // 2], l0.at[d - 1, js], at(x, zd, y, core))
        )
        made.append(wires.copy(dw.at[:, 1, js, xd], l1.at[d - 1, :, js], at(xd, z, y, core)))
    return made


def reduce_part(wires, first, dw, out, l0, l1, s0, s1, m0, m1, swap, x, z, y, core):
    go, started = wires.copy, []
    e, zh = z % 2, z // 2
    wires.got(*first)

    def add0(j, _):
        total = dw[e, 0, j, :, zh].astype(F32)
        for d in range(3):
            total += l0[d, j].astype(F32)
        s0[j] = total.astype(BF)
        for ee in range(2):
            total = dw[ee, 1, j, x].astype(F32)
            for d in range(3):
                total += l1[d, ee, j].astype(F32)
            s1[ee, j] = total.astype(BF)
        return 0

    lax.fori_loop(0, 14, add0, 0)
    for d in range(1, 4):
        zd, xd = (z + d) % 4, (x + d) % 4
        started.append(go(s0.at[:, xd], m0.at[d - 1], at(xd, z, y, core)))
        started.append(go(s1.at[zd % 2, :, zd // 2], m1.at[d - 1], at(x, zd, y, core)))
    wires.got(*started)
    for hf in range(2):
        total = (s0[:, x] if hf == 0 else s1[e, :, zh]).astype(F32)
        got = m0 if hf == 0 else m1
        for d in range(3):
            total += got[d].astype(F32)
        low, high = total[:, :8], total[:, 8:]
        mine = jnp.where(e == 0, low, high).astype(F32)
        other = jnp.where(e == 0, high, low).astype(F32)
        span = pl.ds(14 * hf, 14)
        out[e, span] = jnp.concatenate([mine[:, :, :128], mine[:, :, 128:]], axis=1).astype(BF)
        swap[span] = jnp.concatenate([other[:, :, :128], other[:, :, 128:]], axis=1).astype(BF)
    go(swap, out.at[e], at(x, z + 1 - 2 * e, y, core))


REDUCE_SCRATCH = [
    pltpu.VMEM((3, 14, 4, 16, 256), BF),
    pltpu.VMEM((3, 2, 14, 2, 16, 256), BF),
    pltpu.VMEM((14, 4, 16, 256), BF),
    pltpu.VMEM((2, 14, 2, 16, 256), BF),
    pltpu.VMEM((3, 14, 16, 256), BF),
    pltpu.VMEM((3, 14, 16, 256), BF),
    pltpu.VMEM((28, 16, 128), BF),
]


def shards(tokens, weights, block_rows, grad_hidden):
    wv, brp = views(weights, block_rows)
    tok, wide, ghb, br, out = gather_all(tokens, wv, grad_hidden, brp)
    wide = wide.reshape(8, 4, 14, 128, 256)
    me = lax.axis_index("col").astype(jnp.int32).reshape(1)
    grad_w = out.reshape(4, 14, 2, 8, 128).transpose(0, 1, 3, 2, 4).reshape(4, 14, 8, 256)
    hidden, grad_tok = own_tokens(me, br, tok, wide, ghb)
    return hidden, grad_tok, grad_w


def solution(mesh):
    return jax.shard_map(
        shards,
        mesh=mesh,
        in_specs=(P("row", "col"), P(None, "col", "row", None), P(None, "col"), P("row", "col")),
        out_specs=(P(("row", "col"), None), P(("row", "col"), None), P(None, "col", "row", None)),
        check_vma=False,
    )
```

```python
import jax
import jax.numpy as jnp
from jax import lax
from jax.experimental import pallas as pl
from jax.experimental.pallas import tpu as pltpu
from jax.sharding import PartitionSpec as P

MESH = pl.DeviceIdType.MESH
BF, F32 = jnp.bfloat16, jnp.float32
HBM = pl.BlockSpec(memory_space=pltpu.HBM)
WIRES, LOCALS = 88, 24
VMEM = pl.BlockSpec(memory_space=pltpu.VMEM)


def place():
    row, col = lax.axis_index("row"), lax.axis_index("col")
    return row // 4, row % 4, col // 2, col % 2


def at(x, z, y, core):
    return (x * 4 + z, y * 2 + core)


def greet(peers):
    barrier = pltpu.get_barrier_semaphore()
    for peer in peers:
        pl.semaphore_signal(barrier, inc=1, device_id=peer, device_id_type=MESH)
    pl.semaphore_wait(barrier, len(peers))


class Wires:
    def __init__(self, send, recv):
        self.send, self.recv, self.made = send, recv, 0
        self.unsent, self.ungot = [], []

    def copy(self, src, dst, peer):
        i = self.made
        self.made += 1
        c = pltpu.make_async_remote_copy(
            src_ref=src,
            dst_ref=dst,
            send_sem=self.send.at[i],
            recv_sem=self.recv.at[i],
            device_id=peer,
            device_id_type=MESH,
        )
        c.start()
        self.unsent.append(c)
        self.ungot.append(c)
        return c

    def sent(self, *copies):
        for c in copies:
            self.unsent = [o for o in self.unsent if o is not c]
            c.wait_send()

    def got(self, *copies):
        for c in copies:
            self.ungot = [o for o in self.ungot if o is not c]
            c.wait_recv()

    def finish(self):
        self.got(*list(self.ungot))
        self.sent(*list(self.unsent))


def weight_terms(half, columns, br_ref, tok, own_w, gh, picked, grads, acc, dw):
    def column(j, _):
        rows = [br_ref[k, j] for k in range(4)]
        wide = jnp.concatenate(
            [own_w[k // 2, k % 2, j].reshape(128, 256) for k in range(4)], axis=0
        )
        lane = pl.ds(pl.multiple_of(j * 128, 128), 128)
        for k in range(4):
            picked[:, k * 128 : k * 128 + 128] = tok[rows[k]]
        for t in range(2):
            span = slice(t * 256, t * 256 + 256)
            joined = dot(picked[span], wide, ((1,), (0,)))
            grad = gh[pl.ds(half * 512 + t * 256, 256), lane].astype(F32)
            _, grad_gate, grad_up = swish_parts(joined, grad)
            grads[span, :128] = grad_gate
            grads[span, 128:] = grad_up
        term = dot(picked[...], grads[...], ((0,), (0,)))
        if half == 0:
            acc[j] = term
        else:
            total = (acc[j] + term).astype(BF).reshape(4, 4, 2, 16, 256)
            for k in range(4):
                dw[k // 2, k % 2, j] = total[k]
        return 0

    lax.fori_loop(columns[0], columns[1], column, 0)


def gather_kernel(
    tok_ref, wv_ref, gh_ref, br_ref, rows_ref,
    tokb, wide, ghb, brb, out,
    tok, tokv, wv, wp, slab, own_w, gh, picked, grads, acc, dw,
    l0, l1, s0, s1, m0, m1, swap,
    send, recv, local,
):
    x, z, y, core = place()
    col = y * 2 + core
    e, zh = z % 2, z // 2
    yp, ym, y2 = (y + 1) % 4, (y + 3) % 4, (y + 2) % 4
    zp, zm, z2 = (z + 1) % 4, (z + 3) % 4, (z + 2) % 4
    xp, xm, x2 = (x + 1) % 4, (x + 3) % 4, (x + 2) % 4
    sib = at(x, z, y, 1 - core)
    up, down = at(x, z, yp, core), at(x, z, ym, core)
    cols = [(col + d) % 8 for d in range(1, 8)]
    col_peers = [at(x, z, c // 2, c % 2) for c in cols]
    x_peers = [at(v, z, y, core) for v in (xp, xm, x2)]
    z_peers = [at(x, v, y, core) for v in (zp, zm, z2)]
    wires = Wires(send, recv)
    go, sent, got = wires.copy, wires.sent, wires.got
    locals_made = [0]

    def lcopy(src, dst):
        c = pltpu.make_async_copy(src, dst, local.at[locals_made[0]])
        locals_made[0] += 1
        c.start()
        return c

    def same(part, peer):
        return go(part, part, peer)

    staged = lcopy(tok_ref, tokv)
    own_wv = lcopy(wv_ref.at[e], wv)
    staged.wait()
    own_tok = [
        [
            lcopy(
                tokv.at[pl.ds(512 * r, 512), pl.ds(m * 128, 128)], tok[r].at[col * 8 + m]
            )
            for m in range(8)
        ]
        for r in range(2)
    ]
    own_br = lcopy(br_ref, brb.at[col])
    own_gh = lcopy(gh_ref, gh)
    own_ghb = lcopy(gh_ref.at[pl.ds(pl.multiple_of(col * 128, 128), 128)], ghb.at[col])
    greet(col_peers + x_peers + z_peers)
    pair = go(wv_ref.at[1 - e], wp, at(x, z + 1 - 2 * e, y, core))

    def shard(r, yy, cc):
        return tok[r].at[pl.ds((yy * 2 + cc) * 8, 8)]

    def half_shard(r, yy, h):
        return tok[r].at[pl.ds((yy * 2 + core) * 8 + 4 * h, 4)]

    def start_tokens(r):
        sends = [same(shard(r, y, core), p) for p in (up, down)]
        return sends, [same(shard(r, y, core), sib)]

    def forward_tokens(r, sends, shares):
        got(*sends)
        shares += [same(shard(r, v, core), sib) for v in (ym, yp)]
        return [same(half_shard(r, ym, 0), up), same(half_shard(r, yp, 1), down)]

    def finish_tokens(r, shares, forwards):
        got(*forwards)
        last = same(shard(r, y2, core), sib)
        if r == 1:
            sent(*forwards)
            for c, p in zip(cols, col_peers):
                go(gh_ref.at[pl.ds(pl.multiple_of(c * 128, 128), 128)], ghb.at[col], p)
        got(*shares)
        got(last)

    for c in own_tok[0]:
        c.wait()
    sends0, shares0 = start_tokens(0)
    for c, p in zip(cols, col_peers):
        go(br_ref, brb.at[col], p)
    own_wv.wait()
    got(pair)
    mine, other = wv[...].astype(F32), wp[...].astype(F32)
    low = jnp.where(e == 0, mine, other)
    high = jnp.where(e == 0, other, mine)
    gate = jnp.concatenate([low[:, :8], high[:, :8]], axis=1).astype(BF)
    upper = jnp.concatenate([low[:, 8:], high[:, 8:]], axis=1).astype(BF)
    slab[:, :, :, :128] = gate.reshape(2, 14, 16, 128)
    slab[:, :, :, 128:] = upper.reshape(2, 14, 16, 128)
    ystage = [
        go(slab, wide.at[(y + 4 - v) % 4, core, e, :, :, x, zh], at(x, z, v, core))
        for v in (yp, ym, y2)
    ]
    placed = lcopy(slab, wide.at[0, core, e, :, :, x, zh])
    early = [go(slab.at[0], wide.at[0, core, e, 0, :, x, zh], p) for p in x_peers]
    early += [go(slab.at[1], wide.at[0, core, e, 1, :, x, zh], p) for p in z_peers]
    placed.wait()
    got(*early)
    second = [same(wide.at[0, core, e, 0, :, :, zh], p) for p in z_peers]
    second += [same(wide.at[0, core, :, 1, :, x], p) for p in x_peers]
    got(*ystage)
    others = pl.ds(1, 3)
    first = [same(wide.at[others, core, e, 0, :, x, zh], p) for p in x_peers]
    first += [same(wide.at[others, core, e, 1, :, x, zh], p) for p in z_peers]

    for c in own_tok[1]:
        c.wait()
    forwards0 = forward_tokens(0, sends0, shares0)
    sends1, shares1 = start_tokens(1)
    got(*second)
    own_copy = lcopy(wide.at[0, core], own_w)
    got(*first)

    def w0(zz, js):
        return wide.at[others, core, zz % 2, 0, js, :, zz // 2]

    def w1(xx, js):
        return wide.at[others, core, :, 1, js, xx]

    every, lower, higher = pl.ds(0, 14), pl.ds(0, 7), pl.ds(7, 7)
    zup, zdn = at(x, zp, y, core), at(x, zm, y, core)
    xup, xdn = at(xp, z, y, core), at(xm, z, y, core)
    third = [same(w0(z, every), p) for p in (zup, zdn)] + [same(w1(x, every), p) for p in (xup, xdn)]
    for part in (w0(z, every), w1(x, every)):
        same(part, sib)
    own_copy.wait()
    same(wide.at[0, core], sib)

    finish_tokens(0, shares0, forwards0)
    forwards1 = forward_tokens(1, sends1, shares1)
    own_gh.wait()
    terms = (rows_ref, tok[0], own_w, gh, picked, grads, acc, dw)
    weight_terms(0, (0, 14), *terms)

    got(*third)
    fourth = [same(w0(zm, lower), zup), same(w0(zp, higher), zdn)]
    fourth += [same(w1(xm, lower), xup), same(w1(xp, higher), xdn)]
    for part in (w0(zm, every), w0(zp, every), w1(xm, every), w1(xp, every)):
        same(part, sib)

    finish_tokens(1, shares1, forwards1)
    rows_at = pl.ds(pl.multiple_of(col % 4 * 128, 128), 128)
    keep = [pltpu.make_async_copy(t.at[:, rows_at], tokb, local.at[LOCALS - 1]) for t in tok]
    for h in range(2):
        pl.when(col // 4 == h)(keep[h].start)
    terms = (rows_ref, tok[1], own_w, gh, picked, grads, acc, dw)
    summing = []
    for js in ((0, 7), (7, 14)):
        weight_terms(1, js, *terms)
        summing += reduce_start(wires, js, dw, l0, l1, x, z, y, core)

    got(*fourth)
    for part in (w0(z2, every), w1(x2, every)):
        same(part, sib)
    reduce_part(wires, summing, dw, out, l0, l1, s0, s1, m0, m1, swap, x, z, y, core)
    own_br.wait()
    own_ghb.wait()
    keep[0].wait()
    wires.finish()
    assert (wires.made, locals_made[0]) == (WIRES, LOCALS - 1), (wires.made, locals_made[0])


def gather_all(tokens, wv, grad_hidden, br):
    return pl.pallas_call(
        gather_body,
        out_shape=(
            jax.ShapeDtypeStruct((64, 128, 128), BF),
            jax.ShapeDtypeStruct((4, 2, 2, 2, 14, 4, 2, 16, 256), BF),
            jax.ShapeDtypeStruct((8, 128, 1792), BF),
            jax.ShapeDtypeStruct((8, 4, 14), jnp.int32),
            jax.ShapeDtypeStruct((2, 28, 16, 128), BF),
        ),
        in_specs=[HBM, HBM, HBM, HBM, pl.BlockSpec(memory_space=pltpu.SMEM)],
        out_specs=(HBM, HBM, HBM, HBM, VMEM),
        scratch_shapes=[
            pltpu.VMEM((64, 512, 128), BF),
            pltpu.VMEM((64, 512, 128), BF),
            pltpu.VMEM((1024, 1024), BF),
            pltpu.VMEM((28, 16, 128), BF),
            pltpu.VMEM((28, 16, 128), BF),
            pltpu.VMEM((2, 14, 16, 256), BF),
            pltpu.VMEM((2, 2, 14, 4, 2, 16, 256), BF),
            pltpu.VMEM((1024, 1792), BF),
            pltpu.VMEM((512, 512), BF),
            pltpu.VMEM((512, 256), BF),
            pltpu.VMEM((14, 512, 256), F32),
            pltpu.VMEM((2, 2, 14, 4, 2, 16, 256), BF),
        ]
        + REDUCE_SCRATCH
        + [
            pltpu.SemaphoreType.DMA((WIRES,)),
            pltpu.SemaphoreType.DMA((WIRES,)),
            pltpu.SemaphoreType.DMA((LOCALS,)),
        ],
        compiler_params=pltpu.CompilerParams(
            collective_id=1, has_side_effects=True, vmem_limit_bytes=60 << 20
        ),
        name="gather",
    )(tokens, wv, grad_hidden, br, br)


def gather_body(*refs):
    gather_kernel(*refs[:10], refs[10:12], *refs[12:])


def views(weights, block_rows):
    wv = weights.reshape(4, 14, 8, 2, 128).transpose(0, 1, 3, 2, 4).reshape(2, 28, 16, 128)
    return wv, block_rows


def swish_parts(joined, grad):
    gate, upper = joined[:, :128], joined[:, 128:]
    sig = 1.0 / (1.0 + jnp.exp(-gate))
    act = gate * sig
    grad_gate = grad * upper * sig * (1.0 + gate * (1.0 - sig))
    return (act * upper).astype(BF), grad_gate.astype(BF), (grad * act).astype(BF)


def dot(a, b, dims):
    return lax.dot_general(a, b, (dims, ((), ())), preferred_element_type=F32)


def tokens_kernel(me_ref, br_ref, tok_ref, w_ref, gh_ref, hid_ref, dx_ref, acc, grads):
    step = pl.program_id(0)

    @pl.when(step == 0)
    def _():
        acc[...] = jnp.zeros_like(acc)

    rows = [[br_ref[step, k, j] for k in range(4)] for j in range(14)]
    for j in range(14):
        picked = jnp.concatenate([tok_ref[i] for i in rows[j]], axis=1)
        joined = dot(picked, w_ref[0, :, j].reshape(512, 256), ((1,), (0,)))
        span = slice(j * 128, j * 128 + 128)
        hidden, grad_gate, grad_up = swish_parts(joined, gh_ref[0, :, span].astype(F32))
        hid_ref[:, span] = hidden
        grads[j, :, :128] = grad_gate
        grads[j, :, 128:] = grad_up
    for j in range(14):
        spread = dot(grads[j], w_ref[0, :, j].reshape(512, 256), ((1,), (1,)))
        for k in range(4):
            acc[rows[j][k]] += spread[:, k * 128 : k * 128 + 128]

    @pl.when(step == pl.num_programs(0) - 1)
    def _():
        for b in range(64):
            dx_ref[:, b * 128 : b * 128 + 128] = acc[b].astype(BF)


def relative(s, me, br):
    away = lax.rem(s // 2 - me[0] // 2 + 4, 4)
    return (away * 2 + s % 2, 0, 0, 0, 0)


def own_tokens(me, br, tok, wide, ghb):
    return pl.pallas_call(
        tokens_kernel,
        out_shape=(jax.ShapeDtypeStruct((128, 14336), BF), jax.ShapeDtypeStruct((128, 8192), BF)),
        grid_spec=pltpu.PrefetchScalarGridSpec(
            num_scalar_prefetch=2,
            grid=(8,),
            in_specs=[
                pl.BlockSpec((64, 128, 128), lambda s, me, br: (0, 0, 0)),
                pl.BlockSpec((1, 4, 14, 128, 256), relative),
                pl.BlockSpec((1, 128, 1792), lambda s, me, br: (s, 0, 0)),
            ],
            out_specs=(
                pl.BlockSpec((128, 1792), lambda s, me, br: (0, s)),
                pl.BlockSpec((128, 8192), lambda s, me, br: (0, 0)),
            ),
            scratch_shapes=[pltpu.VMEM((64, 128, 128), F32), pltpu.VMEM((14, 128, 256), BF)],
        ),
        compiler_params=pltpu.CompilerParams(vmem_limit_bytes=62 << 20),
        name="tokens",
    )(me, br, tok, wide, ghb)


def reduce_start(wires, columns, dw, l0, l1, x, z, y, core):
    js, made = pl.ds(columns[0], columns[1] - columns[0]), []
    for d in range(1, 4):
        zd, xd = (z + d) % 4, (x + d) % 4
        made.append(
            wires.copy(dw.at[zd % 2, 0, js, :, zd // 2], l0.at[d - 1, js], at(x, zd, y, core))
        )
        made.append(wires.copy(dw.at[:, 1, js, xd], l1.at[d - 1, :, js], at(xd, z, y, core)))
    return made


def reduce_part(wires, first, dw, out, l0, l1, s0, s1, m0, m1, swap, x, z, y, core):
    go, started = wires.copy, []
    e, zh = z % 2, z // 2
    wires.got(*first)

    def add0(j, _):
        total = dw[e, 0, j, :, zh].astype(F32)
        for d in range(3):
            total += l0[d, j].astype(F32)
        s0[j] = total.astype(BF)
        for ee in range(2):
            total = dw[ee, 1, j, x].astype(F32)
            for d in range(3):
                total += l1[d, ee, j].astype(F32)
            s1[ee, j] = total.astype(BF)
        return 0

    lax.fori_loop(0, 14, add0, 0)
    for d in range(1, 4):
        zd, xd = (z + d) % 4, (x + d) % 4
        started.append(go(s0.at[:, xd], m0.at[d - 1], at(xd, z, y, core)))
        started.append(go(s1.at[zd % 2, :, zd // 2], m1.at[d - 1], at(x, zd, y, core)))
    wires.got(*started)
    for hf in range(2):
        total = (s0[:, x] if hf == 0 else s1[e, :, zh]).astype(F32)
        got = m0 if hf == 0 else m1
        for d in range(3):
            total += got[d].astype(F32)
        low, high = total[:, :8], total[:, 8:]
        mine = jnp.where(e == 0, low, high).astype(F32)
        other = jnp.where(e == 0, high, low).astype(F32)
        span = pl.ds(14 * hf, 14)
        out[e, span] = jnp.concatenate([mine[:, :, :128], mine[:, :, 128:]], axis=1).astype(BF)
        swap[span] = jnp.concatenate([other[:, :, :128], other[:, :, 128:]], axis=1).astype(BF)
    go(swap, out.at[e], at(x, z + 1 - 2 * e, y, core))


REDUCE_SCRATCH = [
    pltpu.VMEM((3, 14, 4, 16, 256), BF),
    pltpu.VMEM((3, 2, 14, 2, 16, 256), BF),
    pltpu.VMEM((14, 4, 16, 256), BF),
    pltpu.VMEM((2, 14, 2, 16, 256), BF),
    pltpu.VMEM((3, 14, 16, 256), BF),
    pltpu.VMEM((3, 14, 16, 256), BF),
    pltpu.VMEM((28, 16, 128), BF),
]


def shards(tokens, weights, block_rows, grad_hidden):
    wv, brp = views(weights, block_rows)
    tok, wide, ghb, br, out = gather_all(tokens, wv, grad_hidden, brp)
    wide = wide.reshape(8, 4, 14, 128, 256)
    me = lax.axis_index("col").astype(jnp.int32).reshape(1)
    grad_w = out.reshape(4, 14, 2, 8, 128).transpose(0, 1, 3, 2, 4).reshape(4, 14, 8, 256)
    hidden, grad_tok = own_tokens(me, br, tok, wide, ghb)
    return hidden, grad_tok, grad_w


def solution(mesh):
    return jax.shard_map(
        shards,
        mesh=mesh,
        in_specs=(P("row", "col"), P(None, "col", "row", None), P(None, "col"), P("row", "col")),
        out_specs=(P(("row", "col"), None), P(("row", "col"), None), P(None, "col", "row", None)),
        check_vma=False,
    )
```

```python
import jax
import jax.numpy as jnp
from jax import lax
from jax.experimental import pallas as pl
from jax.experimental.pallas import tpu as pltpu
from jax.sharding import PartitionSpec as P

MESH = pl.DeviceIdType.MESH
BF, F32 = jnp.bfloat16, jnp.float32
HBM = pl.BlockSpec(memory_space=pltpu.HBM)
WIRES, LOCALS = 88, 24
VMEM = pl.BlockSpec(memory_space=pltpu.VMEM)


def place():
    row, col = lax.axis_index("row"), lax.axis_index("col")
    return row // 4, row % 4, col // 2, col % 2


def at(x, z, y, core):
    return (x * 4 + z, y * 2 + core)


def greet(peers):
    barrier = pltpu.get_barrier_semaphore()
    for peer in peers:
        pl.semaphore_signal(barrier, inc=1, device_id=peer, device_id_type=MESH)
    pl.semaphore_wait(barrier, len(peers))


class Wires:
    def __init__(self, send, recv):
        self.send, self.recv, self.made = send, recv, 0
        self.unsent, self.ungot = [], []

    def copy(self, src, dst, peer):
        i = self.made
        self.made += 1
        c = pltpu.make_async_remote_copy(
            src_ref=src,
            dst_ref=dst,
            send_sem=self.send.at[i],
            recv_sem=self.recv.at[i],
            device_id=peer,
            device_id_type=MESH,
        )
        c.start()
        self.unsent.append(c)
        self.ungot.append(c)
        return c

    def sent(self, *copies):
        for c in copies:
            self.unsent = [o for o in self.unsent if o is not c]
            c.wait_send()

    def got(self, *copies):
        for c in copies:
            self.ungot = [o for o in self.ungot if o is not c]
            c.wait_recv()

    def finish(self):
        self.got(*list(self.ungot))
        self.sent(*list(self.unsent))


def weight_terms(half, columns, br_ref, tok, own_w, gh, picked, grads, acc, dw):
    def column(j, _):
        rows = [br_ref[k, j] for k in range(4)]
        wide = jnp.concatenate(
            [own_w[k // 2, k % 2, j].reshape(128, 256) for k in range(4)], axis=0
        )
        lane = pl.ds(pl.multiple_of(j * 128, 128), 128)
        for k in range(4):
            picked[:, k * 128 : k * 128 + 128] = tok[rows[k]]
        for t in range(2):
            span = slice(t * 256, t * 256 + 256)
            joined = dot(picked[span], wide, ((1,), (0,)))
            grad = gh[pl.ds(half * 512 + t * 256, 256), lane].astype(F32)
            _, grad_gate, grad_up = swish_parts(joined, grad)
            grads[span, :128] = grad_gate
            grads[span, 128:] = grad_up
        term = dot(picked[...], grads[...], ((0,), (0,)))
        if half == 0:
            acc[j] = term
        else:
            total = (acc[j] + term).astype(BF).reshape(4, 4, 2, 16, 256)
            for k in range(4):
                dw[k // 2, k % 2, j] = total[k]
        return 0

    lax.fori_loop(columns[0], columns[1], column, 0)


def gather_kernel(
    tok_ref, wv_ref, gh_ref, br_ref, rows_ref,
    tokb, wide, ghb, brb, out,
    tok, tokv, wv, wp, slab, own_w, gh, picked, grads, acc, dw,
    l0, l1, s0, s1, m0, m1, swap,
    send, recv, local,
):
    x, z, y, core = place()
    col = y * 2 + core
    e, zh = z % 2, z // 2
    yp, ym, y2 = (y + 1) % 4, (y + 3) % 4, (y + 2) % 4
    zp, zm, z2 = (z + 1) % 4, (z + 3) % 4, (z + 2) % 4
    xp, xm, x2 = (x + 1) % 4, (x + 3) % 4, (x + 2) % 4
    sib = at(x, z, y, 1 - core)
    up, down = at(x, z, yp, core), at(x, z, ym, core)
    cols = [(col + d) % 8 for d in range(1, 8)]
    col_peers = [at(x, z, c // 2, c % 2) for c in cols]
    x_peers = [at(v, z, y, core) for v in (xp, xm, x2)]
    z_peers = [at(x, v, y, core) for v in (zp, zm, z2)]
    wires = Wires(send, recv)
    go, sent, got = wires.copy, wires.sent, wires.got
    locals_made = [0]

    def lcopy(src, dst):
        c = pltpu.make_async_copy(src, dst, local.at[locals_made[0]])
        locals_made[0] += 1
        c.start()
        return c

    def same(part, peer):
        return go(part, part, peer)

    staged = lcopy(tok_ref, tokv)
    own_wv = lcopy(wv_ref.at[e], wv)
    staged.wait()
    own_tok = [
        [
            lcopy(
                tokv.at[pl.ds(512 * r, 512), pl.ds(m * 128, 128)], tok[r].at[col * 8 + m]
            )
            for m in range(8)
        ]
        for r in range(2)
    ]
    own_br = lcopy(br_ref, brb.at[col])
    own_gh = lcopy(gh_ref, gh)
    own_ghb = lcopy(gh_ref.at[pl.ds(pl.multiple_of(col * 128, 128), 128)], ghb.at[col])
    greet(col_peers + x_peers + z_peers)
    pair = go(wv_ref.at[1 - e], wp, at(x, z + 1 - 2 * e, y, core))

    def shard(r, yy, cc):
        return tok[r].at[pl.ds((yy * 2 + cc) * 8, 8)]

    def half_shard(r, yy, h):
        return tok[r].at[pl.ds((yy * 2 + core) * 8 + 4 * h, 4)]

    def start_tokens(r):
        sends = [same(shard(r, y, core), p) for p in (up, down)]
        return sends, [same(shard(r, y, core), sib)]

    def forward_tokens(r, sends, shares):
        got(*sends)
        shares += [same(shard(r, v, core), sib) for v in (ym, yp)]
        return [same(half_shard(r, ym, 0), up), same(half_shard(r, yp, 1), down)]

    def finish_tokens(r, shares, forwards):
        got(*forwards)
        last = same(shard(r, y2, core), sib)
        if r == 1:
            sent(*forwards)
            for c, p in zip(cols, col_peers):
                go(gh_ref.at[pl.ds(pl.multiple_of(c * 128, 128), 128)], ghb.at[col], p)
        got(*shares)
        got(last)

    for c in own_tok[0]:
        c.wait()
    sends0, shares0 = start_tokens(0)
    for c, p in zip(cols, col_peers):
        go(br_ref, brb.at[col], p)
    own_wv.wait()
    got(pair)
    mine, other = wv[...].astype(F32), wp[...].astype(F32)
    low = jnp.where(e == 0, mine, other)
    high = jnp.where(e == 0, other, mine)
    gate = jnp.concatenate([low[:, :8], high[:, :8]], axis=1).astype(BF)
    upper = jnp.concatenate([low[:, 8:], high[:, 8:]], axis=1).astype(BF)
    slab[:, :, :, :128] = gate.reshape(2, 14, 16, 128)
    slab[:, :, :, 128:] = upper.reshape(2, 14, 16, 128)
    ystage = [
        go(slab, wide.at[(y + 4 - v) % 4, core, e, :, :, x, zh], at(x, z, v, core))
        for v in (yp, ym, y2)
    ]
    placed = lcopy(slab, wide.at[0, core, e, :, :, x, zh])
    early = [go(slab.at[0], wide.at[0, core, e, 0, :, x, zh], p) for p in x_peers]
    early += [go(slab.at[1], wide.at[0, core, e, 1, :, x, zh], p) for p in z_peers]
    placed.wait()
    got(*early)
    second = [same(wide.at[0, core, e, 0, :, :, zh], p) for p in z_peers]
    second += [same(wide.at[0, core, :, 1, :, x], p) for p in x_peers]
    got(*ystage)
    others = pl.ds(1, 3)
    first = [same(wide.at[others, core, e, 0, :, x, zh], p) for p in x_peers]
    first += [same(wide.at[others, core, e, 1, :, x, zh], p) for p in z_peers]

    for c in own_tok[1]:
        c.wait()
    forwards0 = forward_tokens(0, sends0, shares0)
    sends1, shares1 = start_tokens(1)
    got(*second)
    own_copy = lcopy(wide.at[0, core], own_w)
    got(*first)

    def w0(zz, js):
        return wide.at[others, core, zz % 2, 0, js, :, zz // 2]

    def w1(xx, js):
        return wide.at[others, core, :, 1, js, xx]

    every, lower, higher = pl.ds(0, 14), pl.ds(0, 7), pl.ds(7, 7)
    zup, zdn = at(x, zp, y, core), at(x, zm, y, core)
    xup, xdn = at(xp, z, y, core), at(xm, z, y, core)
    third = [same(w0(z, every), p) for p in (zup, zdn)] + [same(w1(x, every), p) for p in (xup, xdn)]
    for part in (w0(z, every), w1(x, every)):
        same(part, sib)
    own_copy.wait()
    same(wide.at[0, core], sib)

    finish_tokens(0, shares0, forwards0)
    forwards1 = forward_tokens(1, sends1, shares1)
    own_gh.wait()
    terms = (rows_ref, tok[0], own_w, gh, picked, grads, acc, dw)
    weight_terms(0, (0, 14), *terms)

    got(*third)
    fourth = [same(w0(zm, lower), zup), same(w0(zp, higher), zdn)]
    fourth += [same(w1(xm, lower), xup), same(w1(xp, higher), xdn)]
    for part in (w0(zm, every), w0(zp, every), w1(xm, every), w1(xp, every)):
        same(part, sib)

    finish_tokens(1, shares1, forwards1)
    rows_at = pl.ds(pl.multiple_of(col % 4 * 128, 128), 128)
    keep = [pltpu.make_async_copy(t.at[:, rows_at], tokb, local.at[LOCALS - 1]) for t in tok]
    for h in range(2):
        pl.when(col // 4 == h)(keep[h].start)
    terms = (rows_ref, tok[1], own_w, gh, picked, grads, acc, dw)
    summing = []
    for js in ((0, 7), (7, 14)):
        weight_terms(1, js, *terms)
        summing += reduce_start(wires, js, dw, l0, l1, x, z, y, core)

    got(*fourth)
    for part in (w0(z2, every), w1(x2, every)):
        same(part, sib)
    reduce_part(wires, summing, dw, out, l0, l1, s0, s1, m0, m1, swap, x, z, y, core)
    own_br.wait()
    own_ghb.wait()
    keep[0].wait()
    wires.finish()
    assert (wires.made, locals_made[0]) == (WIRES, LOCALS - 1), (wires.made, locals_made[0])


def gather_all(tokens, wv, grad_hidden, br):
    return pl.pallas_call(
        gather_body,
        out_shape=(
            jax.ShapeDtypeStruct((64, 128, 128), BF),
            jax.ShapeDtypeStruct((4, 2, 2, 2, 14, 4, 2, 16, 256), BF),
            jax.ShapeDtypeStruct((8, 128, 1792), BF),
            jax.ShapeDtypeStruct((8, 4, 14), jnp.int32),
            jax.ShapeDtypeStruct((2, 28, 16, 128), BF),
        ),
        in_specs=[HBM, HBM, HBM, HBM, pl.BlockSpec(memory_space=pltpu.SMEM)],
        out_specs=(HBM, HBM, HBM, HBM, VMEM),
        scratch_shapes=[
            pltpu.VMEM((64, 512, 128), BF),
            pltpu.VMEM((64, 512, 128), BF),
            pltpu.VMEM((1024, 1024), BF),
            pltpu.VMEM((28, 16, 128), BF),
            pltpu.VMEM((28, 16, 128), BF),
            pltpu.VMEM((2, 14, 16, 256), BF),
            pltpu.VMEM((2, 2, 14, 4, 2, 16, 256), BF),
            pltpu.VMEM((1024, 1792), BF),
            pltpu.VMEM((512, 512), BF),
            pltpu.VMEM((512, 256), BF),
            pltpu.VMEM((14, 512, 256), F32),
            pltpu.VMEM((2, 2, 14, 4, 2, 16, 256), BF),
        ]
        + REDUCE_SCRATCH
        + [
            pltpu.SemaphoreType.DMA((WIRES,)),
            pltpu.SemaphoreType.DMA((WIRES,)),
            pltpu.SemaphoreType.DMA((LOCALS,)),
        ],
        compiler_params=pltpu.CompilerParams(
            collective_id=1, has_side_effects=True, vmem_limit_bytes=60 << 20
        ),
        name="gather",
    )(tokens, wv, grad_hidden, br, br)


def gather_body(*refs):
    gather_kernel(*refs[:10], refs[10:12], *refs[12:])


def views(weights, block_rows):
    wv = weights.reshape(4, 14, 8, 2, 128).transpose(0, 1, 3, 2, 4).reshape(2, 28, 16, 128)
    return wv, block_rows


def swish_parts(joined, grad):
    gate, upper = joined[:, :128], joined[:, 128:]
    sig = 1.0 / (1.0 + jnp.exp(-gate))
    act = gate * sig
    grad_gate = grad * upper * sig * (1.0 + gate * (1.0 - sig))
    return (act * upper).astype(BF), grad_gate.astype(BF), (grad * act).astype(BF)


def dot(a, b, dims):
    return lax.dot_general(a, b, (dims, ((), ())), preferred_element_type=F32)


def tokens_kernel(me_ref, br_ref, tok_ref, w_ref, gh_ref, hid_ref, dx_ref, acc, grads):
    step = pl.program_id(0)

    @pl.when(step == 0)
    def _():
        acc[...] = jnp.zeros_like(acc)

    rows = [[br_ref[step, k, j] for k in range(4)] for j in range(14)]

    def forward(j):
        picked = jnp.concatenate([tok_ref[i] for i in rows[j]], axis=1)
        return dot(picked, w_ref[0, :, j].reshape(512, 256), ((1,), (0,)))

    def backward(j):
        spread = dot(grads[j], w_ref[0, :, j].reshape(512, 256), ((1,), (1,)))
        for k in range(4):
            acc[rows[j][k]] += spread[:, k * 128 : k * 128 + 128]

    following = forward(0)
    for j in range(14):
        joined = following
        if j < 13:
            following = forward(j + 1)
        span = slice(j * 128, j * 128 + 128)
        hidden, grad_gate, grad_up = swish_parts(joined, gh_ref[0, :, span].astype(F32))
        hid_ref[:, span] = hidden
        grads[j, :, :128] = grad_gate
        grads[j, :, 128:] = grad_up
        if j >= 2:
            backward(j - 2)
    backward(12)
    backward(13)

    @pl.when(step == pl.num_programs(0) - 1)
    def _():
        for b in range(64):
            dx_ref[:, b * 128 : b * 128 + 128] = acc[b].astype(BF)


def relative(s, me, br):
    away = lax.rem(s // 2 - me[0] // 2 + 4, 4)
    return (away * 2 + s % 2, 0, 0, 0, 0)


def own_tokens(me, br, tok, wide, ghb):
    return pl.pallas_call(
        tokens_kernel,
        out_shape=(jax.ShapeDtypeStruct((128, 14336), BF), jax.ShapeDtypeStruct((128, 8192), BF)),
        grid_spec=pltpu.PrefetchScalarGridSpec(
            num_scalar_prefetch=2,
            grid=(8,),
            in_specs=[
                pl.BlockSpec((64, 128, 128), lambda s, me, br: (0, 0, 0)),
                pl.BlockSpec((1, 4, 14, 128, 256), relative),
                pl.BlockSpec((1, 128, 1792), lambda s, me, br: (s, 0, 0)),
            ],
            out_specs=(
                pl.BlockSpec((128, 1792), lambda s, me, br: (0, s)),
                pl.BlockSpec((128, 8192), lambda s, me, br: (0, 0)),
            ),
            scratch_shapes=[pltpu.VMEM((64, 128, 128), F32), pltpu.VMEM((14, 128, 256), BF)],
        ),
        compiler_params=pltpu.CompilerParams(vmem_limit_bytes=62 << 20),
        name="tokens",
    )(me, br, tok, wide, ghb)


def reduce_start(wires, columns, dw, l0, l1, x, z, y, core):
    js, made = pl.ds(columns[0], columns[1] - columns[0]), []
    for d in range(1, 4):
        zd, xd = (z + d) % 4, (x + d) % 4
        made.append(
            wires.copy(dw.at[zd % 2, 0, js, :, zd // 2], l0.at[d - 1, js], at(x, zd, y, core))
        )
        made.append(wires.copy(dw.at[:, 1, js, xd], l1.at[d - 1, :, js], at(xd, z, y, core)))
    return made


def reduce_part(wires, first, dw, out, l0, l1, s0, s1, m0, m1, swap, x, z, y, core):
    go, started = wires.copy, []
    e, zh = z % 2, z // 2
    wires.got(*first)

    def add0(j, _):
        total = dw[e, 0, j, :, zh].astype(F32)
        for d in range(3):
            total += l0[d, j].astype(F32)
        s0[j] = total.astype(BF)
        for ee in range(2):
            total = dw[ee, 1, j, x].astype(F32)
            for d in range(3):
                total += l1[d, ee, j].astype(F32)
            s1[ee, j] = total.astype(BF)
        return 0

    lax.fori_loop(0, 14, add0, 0)
    for d in range(1, 4):
        zd, xd = (z + d) % 4, (x + d) % 4
        started.append(go(s0.at[:, xd], m0.at[d - 1], at(xd, z, y, core)))
        started.append(go(s1.at[zd % 2, :, zd // 2], m1.at[d - 1], at(x, zd, y, core)))
    wires.got(*started)
    for hf in range(2):
        total = (s0[:, x] if hf == 0 else s1[e, :, zh]).astype(F32)
        got = m0 if hf == 0 else m1
        for d in range(3):
            total += got[d].astype(F32)
        low, high = total[:, :8], total[:, 8:]
        mine = jnp.where(e == 0, low, high).astype(F32)
        other = jnp.where(e == 0, high, low).astype(F32)
        span = pl.ds(14 * hf, 14)
        out[e, span] = jnp.concatenate([mine[:, :, :128], mine[:, :, 128:]], axis=1).astype(BF)
        swap[span] = jnp.concatenate([other[:, :, :128], other[:, :, 128:]], axis=1).astype(BF)
    go(swap, out.at[e], at(x, z + 1 - 2 * e, y, core))


REDUCE_SCRATCH = [
    pltpu.VMEM((3, 14, 4, 16, 256), BF),
    pltpu.VMEM((3, 2, 14, 2, 16, 256), BF),
    pltpu.VMEM((14, 4, 16, 256), BF),
    pltpu.VMEM((2, 14, 2, 16, 256), BF),
    pltpu.VMEM((3, 14, 16, 256), BF),
    pltpu.VMEM((3, 14, 16, 256), BF),
    pltpu.VMEM((28, 16, 128), BF),
]


def shards(tokens, weights, block_rows, grad_hidden):
    wv, brp = views(weights, block_rows)
    tok, wide, ghb, br, out = gather_all(tokens, wv, grad_hidden, brp)
    wide = wide.reshape(8, 4, 14, 128, 256)
    me = lax.axis_index("col").astype(jnp.int32).reshape(1)
    grad_w = out.reshape(4, 14, 2, 8, 128).transpose(0, 1, 3, 2, 4).reshape(4, 14, 8, 256)
    hidden, grad_tok = own_tokens(me, br, tok, wide, ghb)
    return hidden, grad_tok, grad_w


def solution(mesh):
    return jax.shard_map(
        shards,
        mesh=mesh,
        in_specs=(P("row", "col"), P(None, "col", "row", None), P(None, "col"), P("row", "col")),
        out_specs=(P(("row", "col"), None), P(("row", "col"), None), P(None, "col", "row", None)),
        check_vma=False,
    )
```

```python
import jax
import jax.numpy as jnp
from jax import lax
from jax.experimental import pallas as pl
from jax.experimental.pallas import tpu as pltpu
from jax.sharding import PartitionSpec as P

MESH = pl.DeviceIdType.MESH
BF, F32 = jnp.bfloat16, jnp.float32
HBM = pl.BlockSpec(memory_space=pltpu.HBM)
WIRES, LOCALS = 89, 24
VMEM = pl.BlockSpec(memory_space=pltpu.VMEM)


def place():
    row, col = lax.axis_index("row"), lax.axis_index("col")
    return row // 4, row % 4, col // 2, col % 2


def at(x, z, y, core):
    return (x * 4 + z, y * 2 + core)


def greet(peers):
    barrier = pltpu.get_barrier_semaphore()
    for peer in peers:
        pl.semaphore_signal(barrier, inc=1, device_id=peer, device_id_type=MESH)
    pl.semaphore_wait(barrier, len(peers))


class Wires:
    def __init__(self, send, recv):
        self.send, self.recv, self.made = send, recv, 0
        self.unsent, self.ungot = [], []

    def copy(self, src, dst, peer):
        i = self.made
        self.made += 1
        c = pltpu.make_async_remote_copy(
            src_ref=src,
            dst_ref=dst,
            send_sem=self.send.at[i],
            recv_sem=self.recv.at[i],
            device_id=peer,
            device_id_type=MESH,
        )
        c.start()
        self.unsent.append(c)
        self.ungot.append(c)
        return c

    def sent(self, *copies):
        for c in copies:
            self.unsent = [o for o in self.unsent if o is not c]
            c.wait_send()

    def got(self, *copies):
        for c in copies:
            self.ungot = [o for o in self.ungot if o is not c]
            c.wait_recv()

    def finish(self):
        self.got(*list(self.ungot))
        self.sent(*list(self.unsent))


def weight_terms(half, columns, br_ref, tok, own_w, gh, picked, grads, acc, dw):
    def column(j, _):
        rows = [br_ref[k, j] for k in range(4)]
        wide = jnp.concatenate(
            [own_w[k // 2, k % 2, j].reshape(128, 256) for k in range(4)], axis=0
        )
        lane = pl.ds(pl.multiple_of(j * 128, 128), 128)
        for k in range(4):
            picked[:, k * 128 : k * 128 + 128] = tok[rows[k]]
        for t in range(2):
            span = slice(t * 256, t * 256 + 256)
            joined = dot(picked[span], wide, ((1,), (0,)))
            grad = gh[pl.ds(half * 512 + t * 256, 256), lane].astype(F32)
            _, grad_gate, grad_up = swish_parts(joined, grad)
            grads[span, :128] = grad_gate
            grads[span, 128:] = grad_up
        term = dot(picked[...], grads[...], ((0,), (0,)))
        if half == 0:
            acc[j] = term
        else:
            total = (acc[j] + term).astype(BF).reshape(4, 4, 2, 16, 256)
            for k in range(4):
                dw[k // 2, k % 2, j] = total[k]
        return 0

    lax.fori_loop(columns[0], columns[1], column, 0)


def gather_kernel(
    tok_ref, wv_ref, gh_ref, br_ref, rows_ref,
    tokb, wide, ghb, brb, out,
    tok, tokv, wv, wp, slab, own_w, gh, picked, grads, acc, dw,
    l0, l1, s0, s1, m0, m1, swap,
    send, recv, local,
):
    x, z, y, core = place()
    col = y * 2 + core
    e, zh = z % 2, z // 2
    yp, ym, y2 = (y + 1) % 4, (y + 3) % 4, (y + 2) % 4
    zp, zm, z2 = (z + 1) % 4, (z + 3) % 4, (z + 2) % 4
    xp, xm, x2 = (x + 1) % 4, (x + 3) % 4, (x + 2) % 4
    sib = at(x, z, y, 1 - core)
    up, down = at(x, z, yp, core), at(x, z, ym, core)
    cols = [(col + d) % 8 for d in range(1, 8)]
    col_peers = [at(x, z, c // 2, c % 2) for c in cols]
    x_peers = [at(v, z, y, core) for v in (xp, xm, x2)]
    z_peers = [at(x, v, y, core) for v in (zp, zm, z2)]
    wires = Wires(send, recv)
    go, sent, got = wires.copy, wires.sent, wires.got
    locals_made = [0]

    def lcopy(src, dst):
        c = pltpu.make_async_copy(src, dst, local.at[locals_made[0]])
        locals_made[0] += 1
        c.start()
        return c

    def same(part, peer):
        return go(part, part, peer)

    staged = lcopy(tok_ref, tokv)
    own_wv = lcopy(wv_ref.at[e], wv)
    staged.wait()
    own_tok = [
        [
            lcopy(
                tokv.at[pl.ds(512 * r, 512), pl.ds(m * 128, 128)], tok[r].at[col * 8 + m]
            )
            for m in range(8)
        ]
        for r in range(2)
    ]
    own_br = lcopy(br_ref, brb.at[col])
    own_gh = lcopy(gh_ref, gh)
    own_ghb = lcopy(gh_ref.at[pl.ds(pl.multiple_of(col * 128, 128), 128)], ghb.at[col])
    greet(col_peers + x_peers + z_peers)
    pair = go(wv_ref.at[1 - e], wp, at(x, z + 1 - 2 * e, y, core))

    def shard(r, yy, cc):
        return tok[r].at[pl.ds((yy * 2 + cc) * 8, 8)]

    def half_shard(r, yy, h):
        return tok[r].at[pl.ds((yy * 2 + core) * 8 + 4 * h, 4)]

    def start_tokens(r):
        sends = [same(shard(r, y, core), p) for p in (up, down)]
        return sends, [same(shard(r, y, core), sib)]

    def forward_tokens(r, sends, shares):
        got(*sends)
        shares += [same(shard(r, v, core), sib) for v in (ym, yp)]
        return [same(half_shard(r, ym, 0), up), same(half_shard(r, yp, 1), down)]

    def finish_tokens(r, shares, forwards):
        got(*forwards)
        last = same(shard(r, y2, core), sib)
        if r == 1:
            sent(*forwards)
            for c, p in zip(cols, col_peers):
                go(gh_ref.at[pl.ds(pl.multiple_of(c * 128, 128), 128)], ghb.at[col], p)
        got(*shares)
        got(last)

    for c in own_tok[0]:
        c.wait()
    sends0, shares0 = start_tokens(0)
    for c, p in zip(cols, col_peers):
        go(br_ref, brb.at[col], p)
    own_wv.wait()
    got(pair)
    mine, other = wv[...].astype(F32), wp[...].astype(F32)
    low = jnp.where(e == 0, mine, other)
    high = jnp.where(e == 0, other, mine)
    gate = jnp.concatenate([low[:, :8], high[:, :8]], axis=1).astype(BF)
    upper = jnp.concatenate([low[:, 8:], high[:, 8:]], axis=1).astype(BF)
    slab[:, :, :, :128] = gate.reshape(2, 14, 16, 128)
    slab[:, :, :, 128:] = upper.reshape(2, 14, 16, 128)
    ystage = [
        go(slab, wide.at[(y + 4 - v) % 4, core, e, :, :, x, zh], at(x, z, v, core))
        for v in (yp, ym)
    ]
    placed = lcopy(slab, wide.at[0, core, e, :, :, x, zh])
    early = [go(slab.at[0], wide.at[0, core, e, 0, :, x, zh], p) for p in x_peers]
    early += [go(slab.at[1], wide.at[0, core, e, 1, :, x, zh], p) for p in z_peers]
    placed.wait()
    got(*early)
    second = [same(wide.at[0, core, e, 0, :, :, zh], p) for p in z_peers]
    second += [same(wide.at[0, core, :, 1, :, x], p) for p in x_peers]
    got(*ystage)
    far = [(3, 0, up), (1, 1, down)]
    ystage = [
        go(wide.at[v, core, e, hf, :, x, zh], wide.at[2, core, e, hf, :, x, zh], p)
        for v, hf, p in far
    ]
    got(*ystage)
    others = pl.ds(1, 3)
    first = [same(wide.at[others, core, e, 0, :, x, zh], p) for p in x_peers]
    first += [same(wide.at[others, core, e, 1, :, x, zh], p) for p in z_peers]

    for c in own_tok[1]:
        c.wait()
    forwards0 = forward_tokens(0, sends0, shares0)
    sends1, shares1 = start_tokens(1)
    got(*second)
    own_copy = lcopy(wide.at[0, core], own_w)
    got(*first)

    def w0(zz, js):
        return wide.at[others, core, zz % 2, 0, js, :, zz // 2]

    def w1(xx, js):
        return wide.at[others, core, :, 1, js, xx]

    every, lower, higher = pl.ds(0, 14), pl.ds(0, 7), pl.ds(7, 7)
    zup, zdn = at(x, zp, y, core), at(x, zm, y, core)
    xup, xdn = at(xp, z, y, core), at(xm, z, y, core)
    third = [same(w0(z, every), p) for p in (zup, zdn)] + [same(w1(x, every), p) for p in (xup, xdn)]
    for part in (w0(z, every), w1(x, every)):
        same(part, sib)
    own_copy.wait()
    same(wide.at[0, core], sib)

    finish_tokens(0, shares0, forwards0)
    forwards1 = forward_tokens(1, sends1, shares1)
    own_gh.wait()
    terms = (rows_ref, tok[0], own_w, gh, picked, grads, acc, dw)
    weight_terms(0, (0, 14), *terms)

    got(*third)
    fourth = [same(w0(zm, lower), zup), same(w0(zp, higher), zdn)]
    fourth += [same(w1(xm, lower), xup), same(w1(xp, higher), xdn)]
    for part in (w0(zm, every), w0(zp, every), w1(xm, every), w1(xp, every)):
        same(part, sib)

    finish_tokens(1, shares1, forwards1)
    rows_at = pl.ds(pl.multiple_of(col % 4 * 128, 128), 128)
    keep = [pltpu.make_async_copy(t.at[:, rows_at], tokb, local.at[LOCALS - 1]) for t in tok]
    for h in range(2):
        pl.when(col // 4 == h)(keep[h].start)
    terms = (rows_ref, tok[1], own_w, gh, picked, grads, acc, dw)
    summing = []
    for js in ((0, 7), (7, 14)):
        weight_terms(1, js, *terms)
        summing += reduce_start(wires, js, dw, l0, l1, x, z, y, core)

    got(*fourth)
    for part in (w0(z2, every), w1(x2, every)):
        same(part, sib)
    reduce_part(wires, summing, dw, out, l0, l1, s0, s1, m0, m1, swap, x, z, y, core)
    own_br.wait()
    own_ghb.wait()
    keep[0].wait()
    wires.finish()
    assert (wires.made, locals_made[0]) == (WIRES, LOCALS - 1), (wires.made, locals_made[0])


def gather_all(tokens, wv, grad_hidden, br):
    return pl.pallas_call(
        gather_body,
        out_shape=(
            jax.ShapeDtypeStruct((64, 128, 128), BF),
            jax.ShapeDtypeStruct((4, 2, 2, 2, 14, 4, 2, 16, 256), BF),
            jax.ShapeDtypeStruct((8, 128, 1792), BF),
            jax.ShapeDtypeStruct((8, 4, 14), jnp.int32),
            jax.ShapeDtypeStruct((2, 28, 16, 128), BF),
        ),
        in_specs=[HBM, HBM, HBM, HBM, pl.BlockSpec(memory_space=pltpu.SMEM)],
        out_specs=(HBM, HBM, HBM, HBM, VMEM),
        scratch_shapes=[
            pltpu.VMEM((64, 512, 128), BF),
            pltpu.VMEM((64, 512, 128), BF),
            pltpu.VMEM((1024, 1024), BF),
            pltpu.VMEM((28, 16, 128), BF),
            pltpu.VMEM((28, 16, 128), BF),
            pltpu.VMEM((2, 14, 16, 256), BF),
            pltpu.VMEM((2, 2, 14, 4, 2, 16, 256), BF),
            pltpu.VMEM((1024, 1792), BF),
            pltpu.VMEM((512, 512), BF),
            pltpu.VMEM((512, 256), BF),
            pltpu.VMEM((14, 512, 256), F32),
            pltpu.VMEM((2, 2, 14, 4, 2, 16, 256), BF),
        ]
        + REDUCE_SCRATCH
        + [
            pltpu.SemaphoreType.DMA((WIRES,)),
            pltpu.SemaphoreType.DMA((WIRES,)),
            pltpu.SemaphoreType.DMA((LOCALS,)),
        ],
        compiler_params=pltpu.CompilerParams(
            collective_id=1, has_side_effects=True, vmem_limit_bytes=60 << 20
        ),
        name="gather",
    )(tokens, wv, grad_hidden, br, br)


def gather_body(*refs):
    gather_kernel(*refs[:10], refs[10:12], *refs[12:])


def views(weights, block_rows):
    wv = weights.reshape(4, 14, 8, 2, 128).transpose(0, 1, 3, 2, 4).reshape(2, 28, 16, 128)
    return wv, block_rows


def swish_parts(joined, grad):
    gate, upper = joined[:, :128], joined[:, 128:]
    sig = 1.0 / (1.0 + jnp.exp(-gate))
    act = gate * sig
    grad_gate = grad * upper * sig * (1.0 + gate * (1.0 - sig))
    return (act * upper).astype(BF), grad_gate.astype(BF), (grad * act).astype(BF)


def dot(a, b, dims):
    return lax.dot_general(a, b, (dims, ((), ())), preferred_element_type=F32)


def tokens_kernel(me_ref, br_ref, tok_ref, w_ref, gh_ref, hid_ref, dx_ref, acc, grads):
    step = pl.program_id(0)

    @pl.when(step == 0)
    def _():
        acc[...] = jnp.zeros_like(acc)

    rows = [[br_ref[step, k, j] for k in range(4)] for j in range(14)]

    def forward(j):
        picked = jnp.concatenate([tok_ref[i] for i in rows[j]], axis=1)
        return dot(picked, w_ref[0, :, j].reshape(512, 256), ((1,), (0,)))

    def backward(j):
        spread = dot(grads[j], w_ref[0, :, j].reshape(512, 256), ((1,), (1,)))
        for k in range(4):
            acc[rows[j][k]] += spread[:, k * 128 : k * 128 + 128]

    following = forward(0)
    for j in range(14):
        joined = following
        if j < 13:
            following = forward(j + 1)
        span = slice(j * 128, j * 128 + 128)
        hidden, grad_gate, grad_up = swish_parts(joined, gh_ref[0, :, span].astype(F32))
        hid_ref[:, span] = hidden
        grads[j, :, :128] = grad_gate
        grads[j, :, 128:] = grad_up
        if j >= 2:
            backward(j - 2)
    backward(12)
    backward(13)

    @pl.when(step == pl.num_programs(0) - 1)
    def _():
        for b in range(64):
            dx_ref[:, b * 128 : b * 128 + 128] = acc[b].astype(BF)


def relative(s, me, br):
    away = lax.rem(s // 2 - me[0] // 2 + 4, 4)
    return (away * 2 + s % 2, 0, 0, 0, 0)


def own_tokens(me, br, tok, wide, ghb):
    return pl.pallas_call(
        tokens_kernel,
        out_shape=(jax.ShapeDtypeStruct((128, 14336), BF), jax.ShapeDtypeStruct((128, 8192), BF)),
        grid_spec=pltpu.PrefetchScalarGridSpec(
            num_scalar_prefetch=2,
            grid=(8,),
            in_specs=[
                pl.BlockSpec((64, 128, 128), lambda s, me, br: (0, 0, 0)),
                pl.BlockSpec((1, 4, 14, 128, 256), relative),
                pl.BlockSpec((1, 128, 1792), lambda s, me, br: (s, 0, 0)),
            ],
            out_specs=(
                pl.BlockSpec((128, 1792), lambda s, me, br: (0, s)),
                pl.BlockSpec((128, 8192), lambda s, me, br: (0, 0)),
            ),
            scratch_shapes=[pltpu.VMEM((64, 128, 128), F32), pltpu.VMEM((14, 128, 256), BF)],
        ),
        compiler_params=pltpu.CompilerParams(vmem_limit_bytes=62 << 20),
        name="tokens",
    )(me, br, tok, wide, ghb)


def reduce_start(wires, columns, dw, l0, l1, x, z, y, core):
    js, made = pl.ds(columns[0], columns[1] - columns[0]), []
    for d in range(1, 4):
        zd, xd = (z + d) % 4, (x + d) % 4
        made.append(
            wires.copy(dw.at[zd % 2, 0, js, :, zd // 2], l0.at[d - 1, js], at(x, zd, y, core))
        )
        made.append(wires.copy(dw.at[:, 1, js, xd], l1.at[d - 1, :, js], at(xd, z, y, core)))
    return made


def reduce_part(wires, first, dw, out, l0, l1, s0, s1, m0, m1, swap, x, z, y, core):
    go, started = wires.copy, []
    e, zh = z % 2, z // 2
    wires.got(*first)

    def add0(j, _):
        total = dw[e, 0, j, :, zh].astype(F32)
        for d in range(3):
            total += l0[d, j].astype(F32)
        s0[j] = total.astype(BF)
        for ee in range(2):
            total = dw[ee, 1, j, x].astype(F32)
            for d in range(3):
                total += l1[d, ee, j].astype(F32)
            s1[ee, j] = total.astype(BF)
        return 0

    lax.fori_loop(0, 14, add0, 0)
    for d in range(1, 4):
        zd, xd = (z + d) % 4, (x + d) % 4
        started.append(go(s0.at[:, xd], m0.at[d - 1], at(xd, z, y, core)))
        started.append(go(s1.at[zd % 2, :, zd // 2], m1.at[d - 1], at(x, zd, y, core)))
    wires.got(*started)
    for hf in range(2):
        total = (s0[:, x] if hf == 0 else s1[e, :, zh]).astype(F32)
        got = m0 if hf == 0 else m1
        for d in range(3):
            total += got[d].astype(F32)
        low, high = total[:, :8], total[:, 8:]
        mine = jnp.where(e == 0, low, high).astype(F32)
        other = jnp.where(e == 0, high, low).astype(F32)
        span = pl.ds(14 * hf, 14)
        out[e, span] = jnp.concatenate([mine[:, :, :128], mine[:, :, 128:]], axis=1).astype(BF)
        swap[span] = jnp.concatenate([other[:, :, :128], other[:, :, 128:]], axis=1).astype(BF)
    go(swap, out.at[e], at(x, z + 1 - 2 * e, y, core))


REDUCE_SCRATCH = [
    pltpu.VMEM((3, 14, 4, 16, 256), BF),
    pltpu.VMEM((3, 2, 14, 2, 16, 256), BF),
    pltpu.VMEM((14, 4, 16, 256), BF),
    pltpu.VMEM((2, 14, 2, 16, 256), BF),
    pltpu.VMEM((3, 14, 16, 256), BF),
    pltpu.VMEM((3, 14, 16, 256), BF),
    pltpu.VMEM((28, 16, 128), BF),
]


def shards(tokens, weights, block_rows, grad_hidden):
    wv, brp = views(weights, block_rows)
    tok, wide, ghb, br, out = gather_all(tokens, wv, grad_hidden, brp)
    wide = wide.reshape(8, 4, 14, 128, 256)
    me = lax.axis_index("col").astype(jnp.int32).reshape(1)
    grad_w = out.reshape(4, 14, 2, 8, 128).transpose(0, 1, 3, 2, 4).reshape(4, 14, 8, 256)
    hidden, grad_tok = own_tokens(me, br, tok, wide, ghb)
    return hidden, grad_tok, grad_w


def solution(mesh):
    return jax.shard_map(
        shards,
        mesh=mesh,
        in_specs=(P("row", "col"), P(None, "col", "row", None), P(None, "col"), P("row", "col")),
        out_specs=(P(("row", "col"), None), P(("row", "col"), None), P(None, "col", "row", None)),
        check_vma=False,
    )
```

```python
import jax
import jax.numpy as jnp
from jax import lax
from jax.experimental import pallas as pl
from jax.experimental.pallas import tpu as pltpu
from jax.sharding import PartitionSpec as P

MESH = pl.DeviceIdType.MESH
BF, F32 = jnp.bfloat16, jnp.float32
HBM = pl.BlockSpec(memory_space=pltpu.HBM)
WIRES, LOCALS = 89, 24
VMEM = pl.BlockSpec(memory_space=pltpu.VMEM)


def place():
    row, col = lax.axis_index("row"), lax.axis_index("col")
    return row // 4, row % 4, col // 2, col % 2


def at(x, z, y, core):
    return (x * 4 + z, y * 2 + core)


def greet(peers):
    barrier = pltpu.get_barrier_semaphore()
    for peer in peers:
        pl.semaphore_signal(barrier, inc=1, device_id=peer, device_id_type=MESH)
    pl.semaphore_wait(barrier, len(peers))


class Wires:
    def __init__(self, send, recv):
        self.send, self.recv, self.made = send, recv, 0
        self.unsent, self.ungot = [], []

    def copy(self, src, dst, peer):
        i = self.made
        self.made += 1
        c = pltpu.make_async_remote_copy(
            src_ref=src,
            dst_ref=dst,
            send_sem=self.send.at[i],
            recv_sem=self.recv.at[i],
            device_id=peer,
            device_id_type=MESH,
        )
        c.start()
        self.unsent.append(c)
        self.ungot.append(c)
        return c

    def sent(self, *copies):
        for c in copies:
            self.unsent = [o for o in self.unsent if o is not c]
            c.wait_send()

    def got(self, *copies):
        for c in copies:
            self.ungot = [o for o in self.ungot if o is not c]
            c.wait_recv()

    def finish(self):
        self.got(*list(self.ungot))
        self.sent(*list(self.unsent))


def weight_terms(half, columns, br_ref, tok, own_w, gh, picked, grads, acc, dw):
    def column(j, _):
        rows = [br_ref[k, j] for k in range(4)]
        wide = jnp.concatenate(
            [own_w[k // 2, k % 2, j].reshape(128, 256) for k in range(4)], axis=0
        )
        lane = pl.ds(pl.multiple_of(j * 128, 128), 128)
        for k in range(4):
            picked[:, k * 128 : k * 128 + 128] = tok[rows[k]]
        for t in range(2):
            span = slice(t * 256, t * 256 + 256)
            joined = dot(picked[span], wide, ((1,), (0,)))
            grad = gh[pl.ds(half * 512 + t * 256, 256), lane].astype(F32)
            _, grad_gate, grad_up = swish_parts(joined, grad)
            grads[span, :128] = grad_gate
            grads[span, 128:] = grad_up
        term = dot(picked[...], grads[...], ((0,), (0,)))
        if half == 0:
            acc[j] = term
        else:
            total = (acc[j] + term).astype(BF).reshape(4, 4, 2, 16, 256)
            for k in range(4):
                dw[k // 2, k % 2, j] = total[k]
        return 0

    lax.fori_loop(columns[0], columns[1], column, 0)


def gather_kernel(
    tok_ref, wv_ref, gh_ref, br_ref, rows_ref,
    tokb, wide, ghb, brb, out,
    tok, tokv, wv, wp, slab, own_w, gh, picked, grads, acc, dw,
    l0, l1, s0, s1, m0, m1, swap,
    send, recv, local,
):
    x, z, y, core = place()
    col = y * 2 + core
    e, zh = z % 2, z // 2
    yp, ym, y2 = (y + 1) % 4, (y + 3) % 4, (y + 2) % 4
    zp, zm, z2 = (z + 1) % 4, (z + 3) % 4, (z + 2) % 4
    xp, xm, x2 = (x + 1) % 4, (x + 3) % 4, (x + 2) % 4
    sib = at(x, z, y, 1 - core)
    up, down = at(x, z, yp, core), at(x, z, ym, core)
    cols = [(col + d) % 8 for d in range(1, 8)]
    col_peers = [at(x, z, c // 2, c % 2) for c in cols]
    x_peers = [at(v, z, y, core) for v in (xp, xm, x2)]
    z_peers = [at(x, v, y, core) for v in (zp, zm, z2)]
    wires = Wires(send, recv)
    go, sent, got = wires.copy, wires.sent, wires.got
    locals_made = [0]

    def lcopy(src, dst):
        c = pltpu.make_async_copy(src, dst, local.at[locals_made[0]])
        locals_made[0] += 1
        c.start()
        return c

    def same(part, peer):
        return go(part, part, peer)

    staged = lcopy(tok_ref, tokv)
    own_wv = lcopy(wv_ref.at[e], wv)
    staged.wait()
    own_tok = [
        [
            lcopy(
                tokv.at[pl.ds(512 * r, 512), pl.ds(m * 128, 128)], tok[r].at[col * 8 + m]
            )
            for m in range(8)
        ]
        for r in range(2)
    ]
    own_br = lcopy(br_ref, brb.at[col])
    own_gh = lcopy(gh_ref, gh)
    own_ghb = lcopy(gh_ref.at[pl.ds(pl.multiple_of(col * 128, 128), 128)], ghb.at[col])
    greet(col_peers + x_peers + z_peers)
    pair = go(wv_ref.at[1 - e], wp, at(x, z + 1 - 2 * e, y, core))

    def shard(r, yy, cc):
        return tok[r].at[pl.ds((yy * 2 + cc) * 8, 8)]

    def half_shard(r, yy, h):
        return tok[r].at[pl.ds((yy * 2 + core) * 8 + 4 * h, 4)]

    def start_tokens(r):
        sends = [same(shard(r, y, core), p) for p in (up, down)]
        return sends, [same(shard(r, y, core), sib)]

    def forward_tokens(r, sends, shares):
        got(*sends)
        forwards = [same(half_shard(r, ym, 0), up), same(half_shard(r, yp, 1), down)]
        shares += [same(shard(r, v, core), sib) for v in (ym, yp)]
        return forwards

    for c in own_tok[0]:
        c.wait()
    sends0, shares0 = start_tokens(0)
    for c, p in zip(cols, col_peers):
        go(br_ref, brb.at[col], p)
    own_wv.wait()
    got(pair)
    mine, other = wv[...].astype(F32), wp[...].astype(F32)
    low = jnp.where(e == 0, mine, other)
    high = jnp.where(e == 0, other, mine)
    gate = jnp.concatenate([low[:, :8], high[:, :8]], axis=1).astype(BF)
    upper = jnp.concatenate([low[:, 8:], high[:, 8:]], axis=1).astype(BF)
    slab[:, :, :, :128] = gate.reshape(2, 14, 16, 128)
    slab[:, :, :, 128:] = upper.reshape(2, 14, 16, 128)
    ystage = [
        go(slab, wide.at[(y + 4 - v) % 4, core, e, :, :, x, zh], at(x, z, v, core))
        for v in (yp, ym)
    ]
    placed = lcopy(slab, wide.at[0, core, e, :, :, x, zh])
    early = [go(slab.at[0], wide.at[0, core, e, 0, :, x, zh], p) for p in x_peers]
    early += [go(slab.at[1], wide.at[0, core, e, 1, :, x, zh], p) for p in z_peers]
    placed.wait()
    got(*early)
    second = [same(wide.at[0, core, e, 0, :, :, zh], p) for p in z_peers]
    second += [same(wide.at[0, core, :, 1, :, x], p) for p in x_peers]
    got(*ystage)
    far = [(3, 0, up), (1, 1, down)]
    ystage = [
        go(wide.at[v, core, e, hf, :, x, zh], wide.at[2, core, e, hf, :, x, zh], p)
        for v, hf, p in far
    ]
    got(*ystage)
    others = pl.ds(1, 3)
    first = [same(wide.at[others, core, e, 0, :, x, zh], p) for p in x_peers]
    first += [same(wide.at[others, core, e, 1, :, x, zh], p) for p in z_peers]

    for c in own_tok[1]:
        c.wait()
    forwards0 = forward_tokens(0, sends0, shares0)
    sends1, shares1 = start_tokens(1)
    got(*second)
    own_copy = lcopy(wide.at[0, core], own_w)
    got(*first)

    def w0(zz, js):
        return wide.at[others, core, zz % 2, 0, js, :, zz // 2]

    def w1(xx, js):
        return wide.at[others, core, :, 1, js, xx]

    every, lower, higher = pl.ds(0, 14), pl.ds(0, 7), pl.ds(7, 7)
    zup, zdn = at(x, zp, y, core), at(x, zm, y, core)
    xup, xdn = at(xp, z, y, core), at(xm, z, y, core)
    third = [same(w0(z, every), p) for p in (zup, zdn)] + [same(w1(x, every), p) for p in (xup, xdn)]
    for part in (w0(z, every), w1(x, every)):
        same(part, sib)
    own_copy.wait()
    same(wide.at[0, core], sib)

    got(*forwards0)
    shares0.append(same(shard(0, y2, core), sib))
    forwards1 = forward_tokens(1, sends1, shares1)
    got(*shares0)
    own_gh.wait()
    terms = (rows_ref, tok[0], own_w, gh, picked, grads, acc, dw)
    weight_terms(0, (0, 14), *terms)

    got(*third)
    fourth = [same(w0(zm, lower), zup), same(w0(zp, higher), zdn)]
    fourth += [same(w1(xm, lower), xup), same(w1(xp, higher), xdn)]
    for part in (w0(zm, every), w0(zp, every), w1(xm, every), w1(xp, every)):
        same(part, sib)

    got(*forwards1)
    shares1.append(same(shard(1, y2, core), sib))
    sent(*forwards1)
    for c, p in zip(cols, col_peers):
        go(gh_ref.at[pl.ds(pl.multiple_of(c * 128, 128), 128)], ghb.at[col], p)
    got(*shares1)
    rows_at = pl.ds(pl.multiple_of(col % 4 * 128, 128), 128)
    keep = [pltpu.make_async_copy(t.at[:, rows_at], tokb, local.at[LOCALS - 1]) for t in tok]
    for h in range(2):
        pl.when(col // 4 == h)(keep[h].start)
    terms = (rows_ref, tok[1], own_w, gh, picked, grads, acc, dw)
    summing = []
    for js in ((0, 7), (7, 14)):
        weight_terms(1, js, *terms)
        summing += reduce_start(wires, js, dw, l0, l1, x, z, y, core)

    got(*fourth)
    for part in (w0(z2, every), w1(x2, every)):
        same(part, sib)
    reduce_part(wires, summing, dw, out, l0, l1, s0, s1, m0, m1, swap, x, z, y, core)
    own_br.wait()
    own_ghb.wait()
    keep[0].wait()
    wires.finish()
    assert (wires.made, locals_made[0]) == (WIRES, LOCALS - 1), (wires.made, locals_made[0])


def gather_all(tokens, wv, grad_hidden, br):
    return pl.pallas_call(
        gather_body,
        out_shape=(
            jax.ShapeDtypeStruct((64, 128, 128), BF),
            jax.ShapeDtypeStruct((4, 2, 2, 2, 14, 4, 2, 16, 256), BF),
            jax.ShapeDtypeStruct((8, 128, 1792), BF),
            jax.ShapeDtypeStruct((8, 4, 14), jnp.int32),
            jax.ShapeDtypeStruct((2, 28, 16, 128), BF),
        ),
        in_specs=[HBM, HBM, HBM, HBM, pl.BlockSpec(memory_space=pltpu.SMEM)],
        out_specs=(HBM, HBM, HBM, HBM, VMEM),
        scratch_shapes=[
            pltpu.VMEM((64, 512, 128), BF),
            pltpu.VMEM((64, 512, 128), BF),
            pltpu.VMEM((1024, 1024), BF),
            pltpu.VMEM((28, 16, 128), BF),
            pltpu.VMEM((28, 16, 128), BF),
            pltpu.VMEM((2, 14, 16, 256), BF),
            pltpu.VMEM((2, 2, 14, 4, 2, 16, 256), BF),
            pltpu.VMEM((1024, 1792), BF),
            pltpu.VMEM((512, 512), BF),
            pltpu.VMEM((512, 256), BF),
            pltpu.VMEM((14, 512, 256), F32),
            pltpu.VMEM((2, 2, 14, 4, 2, 16, 256), BF),
        ]
        + REDUCE_SCRATCH
        + [
            pltpu.SemaphoreType.DMA((WIRES,)),
            pltpu.SemaphoreType.DMA((WIRES,)),
            pltpu.SemaphoreType.DMA((LOCALS,)),
        ],
        compiler_params=pltpu.CompilerParams(
            collective_id=1, has_side_effects=True, vmem_limit_bytes=60 << 20
        ),
        name="gather",
    )(tokens, wv, grad_hidden, br, br)


def gather_body(*refs):
    gather_kernel(*refs[:10], refs[10:12], *refs[12:])


def views(weights, block_rows):
    wv = weights.reshape(4, 14, 8, 2, 128).transpose(0, 1, 3, 2, 4).reshape(2, 28, 16, 128)
    return wv, block_rows


def swish_parts(joined, grad):
    gate, upper = joined[:, :128], joined[:, 128:]
    sig = 1.0 / (1.0 + jnp.exp(-gate))
    act = gate * sig
    grad_gate = grad * upper * sig * (1.0 + gate * (1.0 - sig))
    return (act * upper).astype(BF), grad_gate.astype(BF), (grad * act).astype(BF)


def dot(a, b, dims):
    return lax.dot_general(a, b, (dims, ((), ())), preferred_element_type=F32)


def tokens_kernel(me_ref, br_ref, tok_ref, w_ref, gh_ref, hid_ref, dx_ref, acc, grads):
    step = pl.program_id(0)

    @pl.when(step == 0)
    def _():
        acc[...] = jnp.zeros_like(acc)

    rows = [[br_ref[step, k, j] for k in range(4)] for j in range(14)]

    def forward(j):
        picked = jnp.concatenate([tok_ref[i] for i in rows[j]], axis=1)
        return dot(picked, w_ref[0, :, j].reshape(512, 256), ((1,), (0,)))

    def backward(j):
        spread = dot(grads[j], w_ref[0, :, j].reshape(512, 256), ((1,), (1,)))
        for k in range(4):
            acc[rows[j][k]] += spread[:, k * 128 : k * 128 + 128]

    following = forward(0)
    for j in range(14):
        joined = following
        if j < 13:
            following = forward(j + 1)
        span = slice(j * 128, j * 128 + 128)
        hidden, grad_gate, grad_up = swish_parts(joined, gh_ref[0, :, span].astype(F32))
        hid_ref[:, span] = hidden
        grads[j, :, :128] = grad_gate
        grads[j, :, 128:] = grad_up
        if j >= 2:
            backward(j - 2)
    backward(12)
    backward(13)

    @pl.when(step == pl.num_programs(0) - 1)
    def _():
        for b in range(64):
            dx_ref[:, b * 128 : b * 128 + 128] = acc[b].astype(BF)


def relative(s, me, br):
    away = lax.rem(s // 2 - me[0] // 2 + 4, 4)
    return (away * 2 + s % 2, 0, 0, 0, 0)


def own_tokens(me, br, tok, wide, ghb):
    return pl.pallas_call(
        tokens_kernel,
        out_shape=(jax.ShapeDtypeStruct((128, 14336), BF), jax.ShapeDtypeStruct((128, 8192), BF)),
        grid_spec=pltpu.PrefetchScalarGridSpec(
            num_scalar_prefetch=2,
            grid=(8,),
            in_specs=[
                pl.BlockSpec((64, 128, 128), lambda s, me, br: (0, 0, 0)),
                pl.BlockSpec((1, 4, 14, 128, 256), relative),
                pl.BlockSpec((1, 128, 1792), lambda s, me, br: (s, 0, 0)),
            ],
            out_specs=(
                pl.BlockSpec((128, 1792), lambda s, me, br: (0, s)),
                pl.BlockSpec((128, 8192), lambda s, me, br: (0, 0)),
            ),
            scratch_shapes=[pltpu.VMEM((64, 128, 128), F32), pltpu.VMEM((14, 128, 256), BF)],
        ),
        compiler_params=pltpu.CompilerParams(vmem_limit_bytes=62 << 20),
        name="tokens",
    )(me, br, tok, wide, ghb)


def reduce_start(wires, columns, dw, l0, l1, x, z, y, core):
    js, made = pl.ds(columns[0], columns[1] - columns[0]), []
    for d in range(1, 4):
        zd, xd = (z + d) % 4, (x + d) % 4
        made.append(
            wires.copy(dw.at[zd % 2, 0, js, :, zd // 2], l0.at[d - 1, js], at(x, zd, y, core))
        )
        made.append(wires.copy(dw.at[:, 1, js, xd], l1.at[d - 1, :, js], at(xd, z, y, core)))
    return made


def reduce_part(wires, first, dw, out, l0, l1, s0, s1, m0, m1, swap, x, z, y, core):
    go, started = wires.copy, []
    e, zh = z % 2, z // 2
    wires.got(*first)

    def add0(j, _):
        total = dw[e, 0, j, :, zh].astype(F32)
        for d in range(3):
            total += l0[d, j].astype(F32)
        s0[j] = total.astype(BF)
        for ee in range(2):
            total = dw[ee, 1, j, x].astype(F32)
            for d in range(3):
                total += l1[d, ee, j].astype(F32)
            s1[ee, j] = total.astype(BF)
        return 0

    lax.fori_loop(0, 14, add0, 0)
    for d in range(1, 4):
        zd, xd = (z + d) % 4, (x + d) % 4
        started.append(go(s0.at[:, xd], m0.at[d - 1], at(xd, z, y, core)))
        started.append(go(s1.at[zd % 2, :, zd // 2], m1.at[d - 1], at(x, zd, y, core)))
    wires.got(*started)
    for hf in range(2):
        total = (s0[:, x] if hf == 0 else s1[e, :, zh]).astype(F32)
        got = m0 if hf == 0 else m1
        for d in range(3):
            total += got[d].astype(F32)
        low, high = total[:, :8], total[:, 8:]
        mine = jnp.where(e == 0, low, high).astype(F32)
        other = jnp.where(e == 0, high, low).astype(F32)
        span = pl.ds(14 * hf, 14)
        out[e, span] = jnp.concatenate([mine[:, :, :128], mine[:, :, 128:]], axis=1).astype(BF)
        swap[span] = jnp.concatenate([other[:, :, :128], other[:, :, 128:]], axis=1).astype(BF)
    go(swap, out.at[e], at(x, z + 1 - 2 * e, y, core))


REDUCE_SCRATCH = [
    pltpu.VMEM((3, 14, 4, 16, 256), BF),
    pltpu.VMEM((3, 2, 14, 2, 16, 256), BF),
    pltpu.VMEM((14, 4, 16, 256), BF),
    pltpu.VMEM((2, 14, 2, 16, 256), BF),
    pltpu.VMEM((3, 14, 16, 256), BF),
    pltpu.VMEM((3, 14, 16, 256), BF),
    pltpu.VMEM((28, 16, 128), BF),
]


def shards(tokens, weights, block_rows, grad_hidden):
    wv, brp = views(weights, block_rows)
    tok, wide, ghb, br, out = gather_all(tokens, wv, grad_hidden, brp)
    wide = wide.reshape(8, 4, 14, 128, 256)
    me = lax.axis_index("col").astype(jnp.int32).reshape(1)
    grad_w = out.reshape(4, 14, 2, 8, 128).transpose(0, 1, 3, 2, 4).reshape(4, 14, 8, 256)
    hidden, grad_tok = own_tokens(me, br, tok, wide, ghb)
    return hidden, grad_tok, grad_w


def solution(mesh):
    return jax.shard_map(
        shards,
        mesh=mesh,
        in_specs=(P("row", "col"), P(None, "col", "row", None), P(None, "col"), P("row", "col")),
        out_specs=(P(("row", "col"), None), P(("row", "col"), None), P(None, "col", "row", None)),
        check_vma=False,
    )
```
